32 devices in a mesh: dp: 4 (over z), context: 2 (over x), tensor: 4 (over y, core).
Axes of the slice: x: 2, y: 2, z: 4, core: 2. Of those that a mesh axis runs over, the one named last changes fastest.
Arguments:
- tokens: bfloat16 [2048, 2304], P(('dp', 'context')), may hold values from -6 to 6
- segments: int32 [2048], P(('dp', 'context')), may hold values from 0 to 3, as said below
- w_query: bfloat16 [2304, 2048], P('dp', 'tensor'), as said below
- key_weight: bfloat16 [2304, 1024], P('dp', 'tensor'), may hold values from -0.125 to 0.125
- value_weight: bfloat16 [2304, 1024], P('dp', 'tensor'), may hold values from -0.125 to 0.125
- w_output: bfloat16 [2048, 2304], P('tensor', 'dp'), may hold values from -0.125 to 0.125
- w_gate: bfloat16 [2304, 9216], P('dp', 'tensor'), may hold values from -0.125 to 0.125
- w_up: bfloat16 [2304, 9216], P('dp', 'tensor'), may hold values from -0.125 to 0.125
- w_down: bfloat16 [9216, 2304], P('tensor', 'dp'), may hold values from -0.0625 to 0.0625
- pre_attn_gain: bfloat16 [2304], P('dp'), may hold values from -0.5 to 0.5
- post_attn_gain: bfloat16 [2304], P('dp'), may hold values from -0.5 to 0.5
- pre_ffw_gain: bfloat16 [2304], P('dp'), may hold values from -0.5 to 0.5
- post_ffw_gain: bfloat16 [2304], P('dp'), may hold values from -0.5 to 0.5
- cotangent: bfloat16 [2048, 2304], P(('dp', 'context')), may hold values from -6 to 6
Outputs:
- output: bfloat16 [2048, 2304], P(('dp', 'context'))
- tokens_grad: float32 [2048, 2304], P(('dp', 'context'))
- w_query_grad: float32 [2304, 2048], P(('dp', 'context'), 'tensor')
- w_key_grad: float32 [2304, 1024], P(('dp', 'context'), 'tensor')
- w_value_grad: float32 [2304, 1024], P(('dp', 'context'), 'tensor')
- w_output_grad: float32 [2048, 2304], P('tensor', ('dp', 'context'))
- w_gate_grad: float32 [2304, 9216], P(('dp', 'context'), 'tensor')
- w_up_grad: float32 [2304, 9216], P(('dp', 'context'), 'tensor')
- w_down_grad: float32 [9216, 2304], P('tensor', ('dp', 'context'))
- pre_attn_gain_grad: float32 [2304], P(('dp', 'context'))
- post_attn_gain_grad: float32 [2304], P(('dp', 'context'))
- pre_ffw_gain_grad: float32 [2304], P(('dp', 'context'))
- post_ffw_gain_grad: float32 [2304], P(('dp', 'context'))
The draws below stay inside these ranges and needn't reach their ends.
Inputs may be any that keep to these rules, and one draw needn't show every extreme that they name: `segments`: segment numbers never fall along the packed sequence; each of the 4 documents is a run of one token or more. `w_query`: every entry lies within -48 / sqrt(2304) and 48 / sqrt(2304).
All inputs are finite; a program needn't handle non-finite values.
Results may differ from the reference program's by a relative error of at most 0.017.
The reference program's roundings to bfloat16 on the way count: a program that leaves them out, or rounds other values in their place, can miss the bound.
Values may be sent and summed in bfloat16 or wider, within the bound.
No kernel may reach another device: no remote copies, remote signals or barrier semaphores. Data moves between devices by JAX's collectives and lax.ppermute only.
A program may use at most 256 MiB of HBM per device.

```python
import math
import jax
import jax.numpy as jnp
from jax import lax

MODEL_WIDTH = 2304
FF = 9216
QUERY_HEAD_COUNT = 8
KV_HEAD_COUNT = 4
HEAD_SIZE = 256
SLIDE_WINDOW = 4096
DOCS = 4
TOKENS = 2048


def draw_segments(key, part):
    key = jax.random.fold_in(key, 7)
    length_key, longest_key = jax.random.split(key)
    shorter = jax.random.randint(length_key, (DOCS,), 1, TOKENS // (2 * DOCS) + 1).astype(jnp.int32)
    longest = jax.random.randint(longest_key, (), 0, DOCS).astype(jnp.int32)
    document = jnp.arange(DOCS, dtype=jnp.int32)
    shorter = jnp.where(document == longest, 0, shorter).astype(jnp.int32)
    lengths = jnp.where(document == longest, TOKENS - jnp.sum(shorter), shorter).astype(jnp.int32)
    ending = jnp.cumsum(lengths).astype(jnp.int32)
    places = jnp.arange(TOKENS, dtype=jnp.int32)
    return jnp.sum((places[:, None] >= ending[None, :DOCS - 1]).astype(jnp.int32), axis=1).astype(jnp.int32)


def draw_w_query(key, part):
    key = jax.random.fold_in(key, 11)
    base_key, select_key = jax.random.split(key)
    base = jnp.clip(jax.random.normal(base_key, (MODEL_WIDTH, QUERY_HEAD_COUNT * HEAD_SIZE), jnp.float32), -6.0, 6.0) * MODEL_WIDTH ** (-0.5)
    each_key_head = QUERY_HEAD_COUNT // KV_HEAD_COUNT
    selected = jax.random.randint(select_key, (KV_HEAD_COUNT,), 0, each_key_head).astype(jnp.int32)
    head_number = jnp.arange(QUERY_HEAD_COUNT, dtype=jnp.int32)
    louder = head_number % each_key_head == selected[head_number // each_key_head]
    head_scale = jnp.where(louder, 8.0, 1.0).astype(jnp.float32)
    column_scale = jnp.repeat(head_scale, HEAD_SIZE, total_repeat_length=QUERY_HEAD_COUNT * HEAD_SIZE)
    return (base * column_scale[None, :]).astype(jnp.bfloat16)


def steps_of(key, shape, cuts, smallest, high):
    level = 1.0
    for axis_at, blocks in cuts:
        draws = jax.random.uniform(jax.random.fold_in(jax.random.fold_in(key, 6), axis_at), (blocks,), jnp.float32, smallest / len(cuts), high / len(cuts))
        level = level * jnp.repeat(jnp.exp(draws), shape[axis_at] // blocks).reshape((-1,) + (1,) * (len(shape) - 1 - axis_at))
    return level


def gaussian(key, dims, deviation, most, pieces=(), kind=jnp.bfloat16):
    level = steps_of(key, dims, pieces, -0.22, 0.18) if pieces else 1.0
    array = jax.random.normal(key, dims, jnp.float32) * deviation * level
    return jnp.minimum(jnp.maximum(array, -most), most).astype(kind)


def setup_inputs(seed: int = 0) -> dict:
    streams_of = jax.random.split(jax.random.key(seed), 15)
    return {
        "tokens": gaussian(streams_of[0], (TOKENS, MODEL_WIDTH), 1.0, 6.0, ((0, 8),)),
        "segments": draw_segments(jax.random.fold_in(streams_of[14], 71), 0),
        "w_query": draw_w_query(jax.random.fold_in(streams_of[14], 71), 0),
        "key_weight": gaussian(streams_of[3], (MODEL_WIDTH, KV_HEAD_COUNT * HEAD_SIZE), MODEL_WIDTH ** -0.5, 0.125, ((0, 4), (1, 4))),
        "value_weight": gaussian(streams_of[4], (MODEL_WIDTH, KV_HEAD_COUNT * HEAD_SIZE), MODEL_WIDTH ** -0.5, 0.125, ((0, 4), (1, 4))),
        "w_output": gaussian(streams_of[5], (QUERY_HEAD_COUNT * HEAD_SIZE, MODEL_WIDTH), (QUERY_HEAD_COUNT * HEAD_SIZE) ** -0.5, 0.125, ((0, 4), (1, 4))),
        "w_gate": gaussian(streams_of[6], (MODEL_WIDTH, FF), MODEL_WIDTH ** -0.5, 0.125, ((0, 4), (1, 4))),
        "w_up": gaussian(streams_of[7], (MODEL_WIDTH, FF), MODEL_WIDTH ** -0.5, 0.125, ((0, 4), (1, 4))),
        "w_down": gaussian(streams_of[8], (FF, MODEL_WIDTH), FF ** -0.5, 0.0625, ((0, 4), (1, 4))),
        "pre_attn_gain": jnp.clip(jax.random.uniform(streams_of[9], (MODEL_WIDTH,), jnp.float32, -0.5, 0.5) * steps_of(streams_of[9], (MODEL_WIDTH,), ((0, 4),), -0.4, 0.0), -0.5, 0.5).astype(jnp.bfloat16),
        "post_attn_gain": jnp.clip(jax.random.uniform(streams_of[10], (MODEL_WIDTH,), jnp.float32, -0.5, 0.5) * steps_of(streams_of[10], (MODEL_WIDTH,), ((0, 4),), -0.4, 0.0), -0.5, 0.5).astype(jnp.bfloat16),
        "pre_ffw_gain": jnp.clip(jax.random.uniform(streams_of[11], (MODEL_WIDTH,), jnp.float32, -0.5, 0.5) * steps_of(streams_of[11], (MODEL_WIDTH,), ((0, 4),), -0.4, 0.0), -0.5, 0.5).astype(jnp.bfloat16),
        "post_ffw_gain": jnp.clip(jax.random.uniform(streams_of[12], (MODEL_WIDTH,), jnp.float32, -0.5, 0.5) * steps_of(streams_of[12], (MODEL_WIDTH,), ((0, 4),), -0.4, 0.0), -0.5, 0.5).astype(jnp.bfloat16),
        "cotangent": gaussian(streams_of[13], (TOKENS, MODEL_WIDTH), 1.0, 6.0, ((0, 8),)),
    }


@jax.custom_vjp
def reduced_precision(v):
    return lax.optimization_barrier(v.astype(jnp.bfloat16)).astype(jnp.float32)

@jax.custom_vjp
def reduced_backward(v):
    return v

def low_keep(v):
    return (reduced_precision(v), None)

def low_pass(kept, grad):
    return (grad,)

def back_keep(v):
    return (v, None)

def back_low(kept, grad):
    return (reduced_precision(grad),)
reduced_precision.defvjp(low_keep, low_pass)
reduced_backward.defvjp(back_keep, back_low)
eps = 1e-06
softcap = 50.0
negative = -1e+30

def matrix_product(left, right):
    return jnp.dot(left, right, precision=lax.Precision.HIGHEST, preferred_element_type=jnp.float32)

def rms_norm(value_rows, gain):
    return value_rows * lax.rsqrt(lax.optimization_barrier(jnp.mean(value_rows * value_rows, axis=-1, keepdims=True)) + eps) * (1.0 + gain)

def rotary_tables(positions):
    inverse = 1.0 / 10000.0 ** (jnp.arange(0, HEAD_SIZE, 2, dtype=jnp.float32) / HEAD_SIZE)
    angles = positions.astype(jnp.float32)[:, None] * inverse[None, :]
    return (jnp.cos(angles), jnp.sin(angles))

def apply_rotary(value_rows, cosine_table, sine_table):
    half = value_rows.shape[-1] // 2
    first = value_rows[..., :half]
    second = value_rows[..., half:]
    cos_part = cosine_table[:, None, :]
    sin_part = sine_table[:, None, :]
    return jnp.concatenate([first * cos_part - second * sin_part, second * cos_part + first * sin_part], axis=-1)

def attention(query_rows, key_rows, value_rows, segments):
    grand_total = query_rows.shape[0]
    query_block_size = math.gcd(grand_total, 512)
    span = SLIDE_WINDOW + query_block_size
    padded_keys = jnp.concatenate([jnp.zeros((SLIDE_WINDOW, KV_HEAD_COUNT, HEAD_SIZE), key_rows.dtype), key_rows], axis=0)
    padded_values = jnp.concatenate([jnp.zeros((SLIDE_WINDOW, KV_HEAD_COUNT, HEAD_SIZE), value_rows.dtype), value_rows], axis=0)
    pad_segments = jnp.concatenate([jnp.full((SLIDE_WINDOW,), -1, jnp.int32), segments.astype(jnp.int32)], axis=0)
    grouped_heads = query_rows.reshape(grand_total // query_block_size, query_block_size, KV_HEAD_COUNT, QUERY_HEAD_COUNT // KV_HEAD_COUNT, HEAD_SIZE)
    starts = jnp.arange(grand_total // query_block_size, dtype=jnp.int32) * query_block_size

    def one_block(operands):
        query_block, start = operands
        key_block = lax.dynamic_slice_in_dim(padded_keys, start, span, 0)
        value_block = lax.dynamic_slice_in_dim(padded_values, start, span, 0)
        key_segments = lax.dynamic_slice_in_dim(pad_segments, start, span, 0)
        query_segments = lax.dynamic_slice_in_dim(segments.astype(jnp.int32), start, query_block_size, 0)
        query_pos = start + jnp.arange(query_block_size, dtype=jnp.int32)
        key_pos = start - SLIDE_WINDOW + jnp.arange(span, dtype=jnp.int32)
        valid = (key_pos[None, :] <= query_pos[:, None]) & (query_pos[:, None] - key_pos[None, :] < SLIDE_WINDOW)
        valid = valid & (key_pos[None, :] >= 0) & (key_segments[None, :] == query_segments[:, None])
        raw = reduced_backward(jnp.einsum('qkgd,skd->kgqs', query_block, key_block, precision=lax.Precision.HIGHEST))
        capped = softcap * jnp.tanh(raw / softcap)
        probs = reduced_precision(jax.nn.softmax(jnp.where(valid, capped, negative), axis=-1))
        mixed = jnp.einsum('kgqs,skd->qkgd', probs, value_block, precision=lax.Precision.HIGHEST)
        return reduced_precision(reduced_backward(mixed)).reshape(query_block_size, QUERY_HEAD_COUNT * HEAD_SIZE)
    mixed = lax.map(jax.checkpoint(one_block), (grouped_heads, starts))
    return mixed.reshape(grand_total, QUERY_HEAD_COUNT * HEAD_SIZE)

def layer(inputs, w_query, key_weight, value_weight, w_output, w_gate, w_up, w_down, gain_one, gain_two, gain_three, gain_four, segments):
    grand_total = inputs.shape[0]
    raised_rows = reduced_precision(rms_norm(inputs, gain_one))
    query_pre = reduced_backward(matrix_product(raised_rows, w_query))
    key_unrotated = reduced_backward(matrix_product(raised_rows, key_weight))
    value_rows = reduced_precision(reduced_backward(matrix_product(raised_rows, value_weight))).reshape(grand_total, KV_HEAD_COUNT, HEAD_SIZE)
    cosine_table, sine_table = rotary_tables(jnp.arange(grand_total, dtype=jnp.int32))
    query_rows = reduced_precision(apply_rotary(query_pre.reshape(grand_total, QUERY_HEAD_COUNT, HEAD_SIZE), cosine_table, sine_table) * HEAD_SIZE ** (-0.5))
    key_rows = reduced_precision(apply_rotary(key_unrotated.reshape(grand_total, KV_HEAD_COUNT, HEAD_SIZE), cosine_table, sine_table))
    mixed = attention(query_rows, key_rows, value_rows, segments)
    branch = reduced_backward(matrix_product(mixed, w_output))
    middle = inputs + rms_norm(branch, gain_two)
    fblock = math.gcd(grand_total, 2048)

    def feed(rows_block):
        lifted_two = reduced_precision(rms_norm(rows_block, gain_three))
        gate = reduced_backward(matrix_product(lifted_two, w_gate))
        upper = reduced_backward(matrix_product(lifted_two, w_up))
        hidden = reduced_precision(jax.nn.gelu(gate, approximate=True) * upper)
        down = reduced_backward(matrix_product(hidden, w_down))
        return rows_block + rms_norm(down, gain_four)
    result = lax.map(jax.checkpoint(feed), middle.reshape(grand_total // fblock, fblock, MODEL_WIDTH))
    return result.reshape(grand_total, MODEL_WIDTH)

def reference(tokens, segments, w_query, key_weight, value_weight, w_output, w_gate, w_up, w_down, pre_attn_gain, post_attn_gain, pre_ffw_gain, post_ffw_gain, cotangent):
    floats = (tokens, w_query, key_weight, value_weight, w_output, w_gate, w_up, w_down, pre_attn_gain, post_attn_gain, pre_ffw_gain, post_ffw_gain)
    floats = tuple((item.astype(jnp.float32) for item in floats))

    def forward(*params):
        return layer(*params, segments)
    result, pull = jax.vjp(forward, *floats)
    grads = pull(cotangent.astype(jnp.float32))
    return (result.astype(jnp.bfloat16), grads[0], grads[1], grads[2], grads[3], grads[4], grads[5], grads[6], grads[7], grads[8], grads[9], grads[10], grads[11])
```

```python
import jax
import jax.numpy as jnp
from jax import lax
from jax.sharding import PartitionSpec as P

HEAD_SIZE = 256
SLIDE_WINDOW = 4096


eps = 1e-06
softcap = 50.0
negative = -1e30
f32 = jnp.float32
b16 = jnp.bfloat16


def rms_scale(value_rows):
    return lax.rsqrt(jnp.mean(value_rows * value_rows, axis=-1, keepdims=True) + eps)


def rms_back(grad, normed, scale):
    return scale * (grad - normed * jnp.mean(grad * normed, axis=-1, keepdims=True))


def rotary_tables(positions):
    inverse = 1.0 / 10000.0 ** (jnp.arange(0, HEAD_SIZE, 2, dtype=f32) / HEAD_SIZE)
    angles = positions.astype(f32)[:, None] * inverse[None, :]
    return (jnp.cos(angles), jnp.sin(angles))


def apply_rotary(value_rows, cosine_table, sine_table):
    half = value_rows.shape[-1] // 2
    first, second = value_rows[:, :half], value_rows[:, half:]
    return jnp.concatenate(
        [first * cosine_table - second * sine_table, second * cosine_table + first * sine_table],
        axis=-1,
    )


def rotate_back(grads, cosine_table, sine_table):
    return apply_rotary(grads, cosine_table, -sine_table)


def gated(gate_value, up_value):
    return jax.nn.gelu(gate_value, approximate=True) * up_value


def exchange(blocks, axis):
    return lax.all_to_all(blocks, axis, 0, 0, tiled=True)


def gathered(block, axis):
    count = lax.axis_size(axis)
    return exchange(jnp.broadcast_to(block[None], (count,) + block.shape), axis)


def swapped(value, axis, bit):
    count = lax.axis_size(axis)
    return lax.ppermute(value, axis, [(place, place ^ bit) for place in range(count)])


def shifted(value, axis, steps):
    count = lax.axis_size(axis)
    return lax.ppermute(
        value, axis, [(s, s + steps) for s in range(count) if 0 <= s + steps < count]
    )


def summed(blocks):
    return jnp.sum(blocks.astype(f32), axis=0)


def dot(left, right):
    return jnp.dot(left, right, preferred_element_type=f32)


def dot_nt(left, right):
    return lax.dot_general(left, right, (((1,), (1,)), ((), ())), preferred_element_type=f32)


def dot_tn(left, right):
    return lax.dot_general(left, right, (((0,), (0,)), ((), ())), preferred_element_type=f32)


def spread_rows(block):
    stacked = gathered(block, "dp")[None]
    stacked = jnp.concatenate([stacked, swapped(stacked, "tensor", 2)], axis=0)
    stacked = stacked[:, None]
    other = swapped(stacked, "tensor", 1)
    stacked = jnp.concatenate([stacked, other], axis=1)
    return stacked.reshape((-1,) + block.shape[1:])


def collect_rows(partial, sub):
    n = lax.axis_size("dp")
    width = partial.shape[-1]
    stacked = partial.reshape(2, 2, n, sub, width)
    stacked = stacked[:, 0] + swapped(stacked[:, 1].astype(b16), "tensor", 1).astype(f32)
    stacked = stacked[0] + swapped(stacked[1].astype(b16), "tensor", 2).astype(f32)
    return summed(exchange(stacked.astype(b16), "dp"))


def on_device(
    tokens,
    segments,
    w_query,
    key_weight,
    value_weight,
    w_output,
    w_gate,
    w_up,
    w_down,
    pre_attn_gain,
    post_attn_gain,
    pre_ffw_gain,
    post_ffw_gain,
    cotangent,
):
    n = lax.axis_size("dp")
    place = lax.axis_index("dp")
    side = lax.axis_index("context")
    lane = lax.axis_index("tensor")
    lanes = lax.axis_size("tensor")
    rows, width = tokens.shape
    group = 2 * rows
    sub = rows // lanes
    deep = width // n
    reach = min((SLIDE_WINDOW + group - 2) // group, n - 1)
    is_first = side == 0

    def ordered(own, other, axis):
        return jnp.concatenate(
            [jnp.where(is_first, own, other), jnp.where(is_first, other, own)], axis=axis
        )

    def half_of(value, which, axis):
        size = value.shape[axis] // 2
        low = lax.slice_in_dim(value, 0, size, axis=axis)
        high = lax.slice_in_dim(value, size, 2 * size, axis=axis)
        return jnp.where(which == 0, low, high)

    head_cols = jnp.concatenate(
        [half_of(w_query, side, 1), jnp.where(is_first, key_weight, value_weight)], axis=1
    )
    attn_in = gathered(head_cols, "dp").reshape(width, 2 * HEAD_SIZE)
    gains = gathered(
        jnp.stack([pre_attn_gain, post_attn_gain, pre_ffw_gain, post_ffw_gain]), "dp"
    )
    gains = 1.0 + jnp.swapaxes(gains, 0, 1).reshape(4, width).astype(f32)
    all_segments = gathered(segments, ("dp", "context")).reshape(-1)
    tokens_other = swapped(tokens, "context", 1)
    group_tokens = ordered(tokens, tokens_other, 0).astype(f32)
    w_out = jnp.swapaxes(gathered(half_of(w_output, side, 0), "dp"), 0, 1).reshape(
        HEAD_SIZE, width
    )

    units = w_gate.shape[1] // n

    def own_units(weight):
        blocks = jnp.swapaxes(half_of(weight.reshape(deep, n, units), side, 2), 0, 1)
        mine = exchange(blocks, "dp").reshape(width, units // 2)
        return ordered(mine, swapped(mine, "context", 1), 1)

    gate_w = own_units(w_gate)
    up_w = own_units(w_up)
    blocks = half_of(w_down.reshape(n, units, deep), side, 1)
    mine = jnp.swapaxes(exchange(blocks, "dp"), 0, 1).reshape(units // 2, width)
    down_w = ordered(mine, swapped(mine, "context", 1), 0)

    scale_one = rms_scale(group_tokens)
    normed_one = group_tokens * scale_one
    lifted_one = (normed_one * gains[0]).astype(b16)
    projected = dot(lifted_one, attn_in)
    positions = place * group + jnp.arange(group, dtype=jnp.int32)
    cosine_table, sine_table = rotary_tables(positions)
    queries = (
        apply_rotary(projected[:, :HEAD_SIZE], cosine_table, sine_table) * HEAD_SIZE ** (-0.5)
    ).astype(b16)
    mine = projected[:, HEAD_SIZE:]
    mine = jnp.where(is_first, apply_rotary(mine, cosine_table, sine_table), mine).astype(b16)
    mine = [mine] + [shifted(mine, "dp", steps) for steps in range(1, reach + 1)]
    theirs = [swapped(block, "context", 1) for block in mine]
    mine = jnp.concatenate(mine[::-1], axis=0)
    theirs = jnp.concatenate(theirs[::-1], axis=0)
    keys = jnp.where(is_first, mine, theirs)
    values = jnp.where(is_first, theirs, mine)
    span = (reach + 1) * group
    key_positions = (place - reach) * group + jnp.arange(span, dtype=jnp.int32)
    padded = jnp.concatenate([jnp.full((reach * group,), -1, jnp.int32), all_segments])
    key_segments = lax.dynamic_slice_in_dim(padded, place * group, span)
    query_segments = key_segments[reach * group :]
    valid = (key_positions[None, :] <= positions[:, None]) & (
        positions[:, None] - key_positions[None, :] < SLIDE_WINDOW
    )
    valid = valid & (key_positions[None, :] >= 0)
    valid = valid & (key_segments[None, :] == query_segments[:, None])
    bent = jnp.tanh(dot_nt(queries, keys) / softcap)
    masked = jnp.where(valid, softcap * bent, negative)
    weights = jnp.exp(masked - jnp.max(masked, axis=-1, keepdims=True))
    probs = weights / jnp.sum(weights, axis=-1, keepdims=True)
    probs_low = probs.astype(b16)
    mixed = dot(probs_low, values).astype(b16)
    branch = dot(mixed, w_out).astype(b16)
    branch = summed(exchange(branch.reshape(2 * lanes, sub, width), ("context", "tensor")))

    own_tokens = lax.dynamic_slice_in_dim(tokens, lane * sub, sub).astype(f32)
    grad_out = lax.dynamic_slice_in_dim(cotangent, lane * sub, sub).astype(f32)
    scale_two = rms_scale(branch)
    normed_two = branch * scale_two
    middle = own_tokens + normed_two * gains[1]
    scale_three = rms_scale(middle)
    normed_three = middle * scale_three
    lifted_two = spread_rows((normed_three * gains[2]).astype(b16))
    gate = dot(lifted_two, gate_w)
    upper = dot(lifted_two, up_w)
    hidden = gated(gate, upper).astype(b16)
    down = collect_rows(dot(hidden, down_w), sub)
    scale_four = rms_scale(down)
    normed_four = down * scale_four
    output = (middle + normed_four * gains[3]).astype(b16)
    output = gathered(output, "tensor").reshape(rows, width)

    grad_gain_four = jnp.sum(grad_out * normed_four, axis=0)
    grad_down = spread_rows(rms_back(grad_out * gains[3], normed_four, scale_four).astype(b16))
    grad_hidden = dot_nt(grad_down, down_w)
    unused, pull = jax.vjp(gated, gate, upper)
    grad_gate, grad_upper = pull(grad_hidden)
    grad_gate = grad_gate.astype(b16)
    grad_upper = grad_upper.astype(b16)
    lifted_grad = collect_rows(dot_nt(grad_gate, gate_w) + dot_nt(grad_upper, up_w), sub)

    def weight_grad(left, right):
        partial = dot_tn(left, right).reshape(n, 2, deep // 2, units)
        kept = jnp.where(is_first, partial[:, 0], partial[:, 1])
        sent = jnp.where(is_first, partial[:, 1], partial[:, 0])
        total = kept + swapped(sent.astype(b16), "context", 1).astype(f32)
        return exchange(total.astype(b16), "dp")

    grad_w_down = weight_grad(grad_down, hidden)
    grad_w_gate = weight_grad(lifted_two, grad_gate)
    grad_w_up = weight_grad(lifted_two, grad_upper)
    grad_w_down = jnp.swapaxes(grad_w_down, 1, 2).reshape(n * units, deep // 2).astype(f32)
    grad_w_gate = jnp.swapaxes(grad_w_gate, 0, 1).reshape(deep // 2, n * units).astype(f32)
    grad_w_up = jnp.swapaxes(grad_w_up, 0, 1).reshape(deep // 2, n * units).astype(f32)

    grad_gain_three = jnp.sum(lifted_grad * normed_three, axis=0)
    grad_middle = grad_out + rms_back(lifted_grad * gains[2], normed_three, scale_three)
    grad_gain_two = jnp.sum(grad_middle * normed_two, axis=0)
    grad_branch = rms_back(grad_middle * gains[1], normed_two, scale_two).astype(b16)
    grad_branch = gathered(grad_branch, ("context", "tensor")).reshape(group, width)

    grad_w_out = dot_tn(mixed, grad_branch)
    grad_mixed = dot_nt(grad_branch, w_out).astype(b16)
    grad_probs = dot_nt(grad_mixed, values)
    grad_capped = probs * (grad_probs - jnp.sum(probs * grad_probs, axis=-1, keepdims=True))
    grad_raw = (grad_capped * (1.0 - bent * bent)).astype(b16)
    grad_queries = dot(grad_raw, keys)
    grad_keys = dot_tn(grad_raw, queries)
    grad_values = dot_tn(probs_low, grad_mixed)
    kept = jnp.where(is_first, grad_keys, grad_values)
    sent = jnp.where(is_first, grad_values, grad_keys).astype(b16)
    kept = kept + swapped(sent, "context", 1).astype(f32)
    kept = kept.reshape(reach + 1, group, HEAD_SIZE)
    mine = kept[reach]
    for steps in range(1, reach + 1):
        mine = mine + shifted(kept[reach - steps].astype(b16), "dp", -steps).astype(f32)
    grad_query_pre = rotate_back(grad_queries, cosine_table, sine_table) * HEAD_SIZE ** (-0.5)
    mine = jnp.where(is_first, rotate_back(mine, cosine_table, sine_table), mine)
    grad_projected = jnp.concatenate([grad_query_pre, mine], axis=1).astype(b16)
    first_grad = dot_nt(grad_projected, attn_in).astype(b16)
    first_grad = summed(
        exchange(first_grad.reshape(2 * lanes, sub, width), ("context", "tensor"))
    )
    own_scale = rms_scale(own_tokens)
    own_normed = own_tokens * own_scale
    grad_gain_one = jnp.sum(first_grad * own_normed, axis=0)
    grad_inputs = grad_middle + rms_back(first_grad * gains[0], own_normed, own_scale)
    grad_inputs = gathered(grad_inputs.astype(b16), "tensor").reshape(rows, width).astype(f32)

    grad_attn_in = dot_tn(lifted_one, grad_projected).astype(b16)
    grad_attn_in = summed(exchange(grad_attn_in.reshape(n, deep, 2 * HEAD_SIZE), "dp"))
    kept = half_of(grad_attn_in, side, 0)
    got = swapped(half_of(grad_attn_in, 1 - side, 0).astype(b16), "context", 1).astype(f32)
    grad_w_query = ordered(kept[:, :HEAD_SIZE], got[:, :HEAD_SIZE], 1)
    grad_w_key = jnp.where(is_first, kept[:, HEAD_SIZE:], got[:, HEAD_SIZE:])
    grad_w_value = jnp.where(is_first, got[:, HEAD_SIZE:], kept[:, HEAD_SIZE:])
    grad_w_out = jnp.swapaxes(grad_w_out.astype(b16).reshape(HEAD_SIZE, n, deep), 0, 1)
    grad_w_out = summed(exchange(grad_w_out, "dp"))
    kept = half_of(grad_w_out, side, 1)
    got = swapped(half_of(grad_w_out, 1 - side, 1).astype(b16), "context", 1).astype(f32)
    grad_w_out = ordered(kept, got, 0)

    grad_gains = jnp.stack([grad_gain_one, grad_gain_two, grad_gain_three, grad_gain_four])
    grad_gains = jnp.swapaxes(grad_gains.reshape(4, 2 * n, deep // 2), 0, 1)
    grad_gains = jnp.sum(exchange(grad_gains, ("dp", "context")), axis=0)
    grad_gains = jnp.sum(gathered(grad_gains, "tensor"), axis=0)
    return (
        output,
        grad_inputs,
        grad_w_query,
        grad_w_key,
        grad_w_value,
        grad_w_out,
        grad_w_gate,
        grad_w_up,
        grad_w_down,
        grad_gains[0],
        grad_gains[1],
        grad_gains[2],
        grad_gains[3],
    )


def solution(mesh):
    return jax.shard_map(
        on_device,
        mesh=mesh,
        in_specs=(
            P(("dp", "context"), None),
            P(("dp", "context")),
            P("dp", "tensor"),
            P("dp", "tensor"),
            P("dp", "tensor"),
            P("tensor", "dp"),
            P("dp", "tensor"),
            P("dp", "tensor"),
            P("tensor", "dp"),
            P("dp"),
            P("dp"),
            P("dp"),
            P("dp"),
            P(("dp", "context"), None),
        ),
        out_specs=(
            P(("dp", "context"), None),
            P(("dp", "context"), None),
            P(("dp", "context"), "tensor"),
            P(("dp", "context"), "tensor"),
            P(("dp", "context"), "tensor"),
            P("tensor", ("dp", "context")),
            P(("dp", "context"), "tensor"),
            P(("dp", "context"), "tensor"),
            P("tensor", ("dp", "context")),
            P(("dp", "context")),
            P(("dp", "context")),
            P(("dp", "context")),
            P(("dp", "context")),
        ),
        check_vma=False,
    )
```

```python
import jax
import jax.numpy as jnp
from jax import lax
from jax.sharding import PartitionSpec as P

HEAD_SIZE = 256
SLIDE_WINDOW = 4096


eps = 1e-06
softcap = 50.0
negative = -1e30
f32 = jnp.float32
b16 = jnp.bfloat16


def rms_scale(value_rows):
    return lax.rsqrt(jnp.mean(value_rows * value_rows, axis=-1, keepdims=True) + eps)


def rms_back(grad, normed, scale):
    return scale * (grad - normed * jnp.mean(grad * normed, axis=-1, keepdims=True))


def rotary_tables(positions):
    inverse = 1.0 / 10000.0 ** (jnp.arange(0, HEAD_SIZE, 2, dtype=f32) / HEAD_SIZE)
    angles = positions.astype(f32)[:, None] * inverse[None, :]
    return (jnp.cos(angles), jnp.sin(angles))


def apply_rotary(value_rows, cosine_table, sine_table):
    half = value_rows.shape[-1] // 2
    first, second = value_rows[:, :half], value_rows[:, half:]
    return jnp.concatenate(
        [first * cosine_table - second * sine_table, second * cosine_table + first * sine_table],
        axis=-1,
    )


def rotate_back(grads, cosine_table, sine_table):
    return apply_rotary(grads, cosine_table, -sine_table)


def gated(gate_value, up_value):
    return jax.nn.gelu(gate_value, approximate=True) * up_value


def exchange(blocks, axis):
    return lax.all_to_all(blocks, axis, 0, 0, tiled=True)


def gathered(block, axis):
    count = lax.axis_size(axis)
    return exchange(jnp.broadcast_to(block[None], (count,) + block.shape), axis)


def swapped(value, axis, bit):
    count = lax.axis_size(axis)
    return lax.ppermute(value, axis, [(place, place ^ bit) for place in range(count)])


def passed_on(value, steps, way):
    n = lax.axis_size("dp")
    pairs = [(s, s + 1) for s in range(steps - 1, n - 1)]
    if way < 0:
        pairs = [(n - 1 - s, n - 1 - t) for s, t in pairs]
    return lax.ppermute(value, "dp", pairs)


def shifted(value, axis, steps):
    count = lax.axis_size(axis)
    return lax.ppermute(
        value, axis, [(s, s + steps) for s in range(count) if 0 <= s + steps < count]
    )


def summed(blocks):
    return jnp.sum(blocks.astype(f32), axis=0)


def dot(left, right):
    return jnp.dot(left, right, preferred_element_type=f32)


def dot_nt(left, right):
    return lax.dot_general(left, right, (((1,), (1,)), ((), ())), preferred_element_type=f32)


def dot_tn(left, right):
    return lax.dot_general(left, right, (((0,), (0,)), ((), ())), preferred_element_type=f32)


def rotated(value, steps):
    n = lax.axis_size("dp")
    return lax.ppermute(value, "dp", [(s, (s + steps) % n) for s in range(n)])


def picked(first, pair):
    low, high = pair
    return jnp.where(first, low, high), jnp.where(first, high, low)


def after(value, *earlier):
    return lax.optimization_barrier((value,) + earlier)[0]


def bits():
    lane = lax.axis_index("tensor")
    return lax.axis_index("context") == 0, lane < 2, lane % 2 == 0


AXES = (("context", 1), ("tensor", 2), ("tensor", 1))


def join(own, step, axis):
    low, high = picked(bits()[step], (own, swapped(own, *AXES[step])))
    return jnp.stack([low, high], axis=axis)


def fold(partial, step, axis):
    low = lax.index_in_dim(partial, 0, axis, keepdims=False)
    high = lax.index_in_dim(partial, 1, axis, keepdims=False)
    kept, sent = picked(bits()[step], (low, high))
    return kept + swapped(sent.astype(b16), *AXES[step]).astype(f32)


def collect_group(partial, sub):
    width = partial.shape[-1]
    partial = fold(partial.reshape(2, 2, 2, sub, width), 2, 2)
    left, right = partial[..., : width // 2], partial[..., width // 2 :]
    left = fold(fold(left, 0, 0), 1, 0)
    right = fold(fold(right, 1, 1), 0, 0)
    return jnp.concatenate([left, right], axis=-1)


def spread_group(block):
    width = block.shape[-1]
    left, right = block[:, : width // 2], block[:, width // 2 :]
    left = join(join(left, 0, 0), 1, 1)
    right = join(join(right, 1, 0), 0, 0)
    whole = join(jnp.concatenate([left, right], axis=-1), 2, 2)
    return whole.reshape(-1, width)


def spread_lanes(block):
    return join(join(block, 1, 0), 2, 1).reshape(-1, block.shape[-1])


def spread_chunk(block):
    block = jnp.concatenate([block, swapped(block, "tensor", 2)], axis=0)
    return jnp.concatenate([block, swapped(block, "tensor", 1)], axis=0)


def collect_chunk(partial):
    half = partial.shape[0] // 2
    partial = partial[:half] + swapped(partial[half:].astype(b16), "tensor", 1).astype(f32)
    half = half // 2
    return partial[:half] + swapped(partial[half:].astype(b16), "tensor", 2).astype(f32)


def on_device(
    tokens,
    segments,
    w_query,
    key_weight,
    value_weight,
    w_output,
    w_gate,
    w_up,
    w_down,
    pre_attn_gain,
    post_attn_gain,
    pre_ffw_gain,
    post_ffw_gain,
    cotangent,
):
    n = lax.axis_size("dp")
    place = lax.axis_index("dp")
    side = lax.axis_index("context")
    lane = lax.axis_index("tensor")
    lanes = lax.axis_size("tensor")
    rows, width = tokens.shape
    group = 2 * rows
    sub = rows // lanes
    deep = width // n
    reach = min((SLIDE_WINDOW + group - 2) // group, n - 1)
    is_first = side == 0

    def half_of(value, which, axis):
        size = value.shape[axis] // 2
        low = lax.slice_in_dim(value, 0, size, axis=axis)
        high = lax.slice_in_dim(value, size, 2 * size, axis=axis)
        return jnp.where(which == 0, low, high)

    def with_rider(block, values):
        rider = jnp.zeros((16 * HEAD_SIZE - values.size,), b16)
        rider = jnp.concatenate([values.astype(b16).reshape(-1), rider])
        return jnp.concatenate([block, rider.reshape(16, HEAD_SIZE)], axis=0)

    def split_rider(blocks, count):
        size = blocks.shape[1] - 16
        rider = blocks[:, size:].reshape(blocks.shape[0], -1)[:, :count]
        return blocks[:, :size], rider

    gains = jnp.concatenate([pre_attn_gain, post_attn_gain, pre_ffw_gain, post_ffw_gain])
    pair_got = gathered(
        with_rider(jnp.where(is_first, key_weight, value_weight), gains), "dp"
    )
    group_tokens = join(tokens, 0, 0).reshape(group, width).astype(f32)
    segment_pair = join(segments[None].astype(b16), 0, 0)
    pair_in, gains = split_rider(pair_got, 4 * deep)
    pair_in = pair_in.reshape(width, HEAD_SIZE)
    gains = 1.0 + jnp.swapaxes(gains.reshape(n, 4, deep), 0, 1).reshape(4, width).astype(f32)
    query_got = gathered(
        after(with_rider(half_of(w_query, side, 1), segment_pair), pair_got), "dp"
    )
    query_in, all_segments = split_rider(query_got, group)
    query_in = query_in.reshape(width, HEAD_SIZE)
    all_segments = all_segments.reshape(-1).astype(jnp.int32)
    w_out_got = gathered(after(half_of(w_output, side, 0), query_got), "dp")
    w_out = jnp.swapaxes(w_out_got, 0, 1).reshape(HEAD_SIZE, width)

    units = w_gate.shape[1] // n

    def unit_blocks(weight):
        return jnp.swapaxes(half_of(weight, side, 0).reshape(deep // 2, n, units), 0, 1)

    gate_blocks = unit_blocks(after(w_gate, pair_got))
    up_blocks = unit_blocks(after(w_up, pair_got))
    down_blocks = half_of(after(w_down, pair_got).reshape(n, units, deep), side, 1)
    gate_got = exchange(after(gate_blocks, w_out_got), "dp")
    up_got = exchange(after(up_blocks, gate_got), "dp")
    down_got = exchange(after(down_blocks, up_got), "dp")
    gate_w = join(gate_got, 0, 1).reshape(width, units)
    up_w = join(after(up_got, gate_w), 0, 1).reshape(width, units)
    down_half = jnp.swapaxes(after(down_got, up_w), 0, 1).reshape(units // 2, width)
    down_w = join(down_half, 0, 0).reshape(units, width)

    scale_one = rms_scale(group_tokens)
    normed_one = group_tokens * scale_one
    lifted_one = (normed_one * gains[0]).astype(b16)
    positions = place * group + jnp.arange(group, dtype=jnp.int32)
    cosine_table, sine_table = rotary_tables(positions)
    mine = dot(lifted_one, pair_in)
    mine = jnp.where(is_first, apply_rotary(mine, cosine_table, sine_table), mine).astype(b16)
    mine = [mine] + [shifted(mine, "dp", steps) for steps in range(1, reach + 1)]
    theirs = [swapped(block, "context", 1) for block in mine]
    mine[0] = after(mine[0], gate_blocks, up_blocks, down_blocks)
    mine = jnp.concatenate(mine[::-1], axis=0)
    theirs = jnp.concatenate(theirs[::-1], axis=0)
    keys = jnp.where(is_first, mine, theirs)
    values = jnp.where(is_first, theirs, mine)
    queries = (
        apply_rotary(dot(lifted_one, query_in), cosine_table, sine_table) * HEAD_SIZE ** (-0.5)
    ).astype(b16)
    span = (reach + 1) * group
    key_positions = (place - reach) * group + jnp.arange(span, dtype=jnp.int32)
    padded = jnp.concatenate([jnp.full((reach * group,), -1, jnp.int32), all_segments])
    key_segments = lax.dynamic_slice_in_dim(padded, place * group, span)
    query_segments = key_segments[reach * group :]
    valid = (key_positions[None, :] <= positions[:, None]) & (
        positions[:, None] - key_positions[None, :] < SLIDE_WINDOW
    )
    valid = valid & (key_positions[None, :] >= 0)
    valid = valid & (key_segments[None, :] == query_segments[:, None])
    bent = jnp.tanh(dot_nt(queries, keys) / softcap)
    masked = jnp.where(valid, softcap * bent, negative)
    weights = jnp.exp(masked - jnp.max(masked, axis=-1, keepdims=True))
    probs = weights / jnp.sum(weights, axis=-1, keepdims=True)
    probs_low = probs.astype(b16)
    mixed = dot(after(probs_low, w_out_got), values).astype(b16)
    branch = collect_group(dot(mixed, w_out), sub)
    branch = after(branch, gate_got)

    own_tokens = lax.dynamic_slice_in_dim(tokens, lane * sub, sub).astype(f32)
    grad_out = lax.dynamic_slice_in_dim(cotangent, lane * sub, sub).astype(f32)
    scale_two = rms_scale(branch)
    normed_two = branch * scale_two
    middle = own_tokens + normed_two * gains[1]
    scale_three = rms_scale(middle)
    normed_three = middle * scale_three
    lifted_two = (normed_three * gains[2]).astype(b16)
    lifted_two = after(lifted_two, up_got, gate_w)
    lifted_two = [lifted_two] + [
        rotated(after(lifted_two, down_got), steps) for steps in range(1, n)
    ]
    lifted_two = [spread_chunk(block) for block in lifted_two]
    lifted_two[0] = after(lifted_two[0], up_w, down_got)
    gate = [dot(chunk, gate_w) for chunk in lifted_two]
    upper = [dot(chunk, up_w) for chunk in lifted_two]
    hidden = [gated(*pair).astype(b16) for pair in zip(gate, upper)]
    down = [collect_chunk(dot(chunk, down_w)) for chunk in hidden]
    down = down[0] + sum(
        rotated(down[steps].astype(b16), -steps).astype(f32) for steps in range(1, n)
    )
    scale_four = rms_scale(down)
    normed_four = down * scale_four
    output = (middle + normed_four * gains[3]).astype(b16)

    def unit_grad(left, right):
        partial = dot_tn(jnp.concatenate(left, axis=0), jnp.concatenate(right, axis=0))
        return fold(partial.reshape(n, 2, deep // 2, units), 0, 1).astype(b16)

    grad_down = rms_back(grad_out * gains[3], normed_four, scale_four).astype(b16)
    grad_down = [grad_down] + [rotated(grad_down, steps) for steps in range(1, n)]
    grad_down = [spread_chunk(block) for block in grad_down]
    output = spread_lanes(after(output, *grad_down))
    grad_gate, grad_upper, lifted_grad = [], [], []
    for steps in range(n):
        unused, pull = jax.vjp(gated, gate[steps], upper[steps])
        pair = [side.astype(b16) for side in pull(dot_nt(grad_down[steps], down_w))]
        grad_gate.append(pair[0])
        grad_upper.append(pair[1])
        lifted_grad.append(collect_chunk(dot_nt(pair[0], gate_w) + dot_nt(pair[1], up_w)))
    down_part = unit_grad(grad_down, hidden)
    grad_gate[0] = after(grad_gate[0], *lifted_grad)
    gate_part = unit_grad(lifted_two, grad_gate)
    lifted_grad = lifted_grad[0] + sum(
        rotated(lifted_grad[steps].astype(b16), -steps).astype(f32) for steps in range(1, n)
    )
    lifted_grad = after(lifted_grad, down_part)
    grad_middle = grad_out + rms_back(lifted_grad * gains[2], normed_three, scale_three)
    grad_branch = rms_back(grad_middle * gains[1], normed_two, scale_two).astype(b16)
    grad_branch = after(grad_branch, gate_part, output)
    grad_w_down = exchange(after(down_part, grad_branch), "dp")
    grad_upper[0] = after(grad_upper[0], grad_branch)
    up_part = unit_grad(lifted_two, grad_upper)
    grad_branch = spread_group(grad_branch)

    grad_branch = after(grad_branch, grad_w_down, up_part)
    grad_w_gate = exchange(after(gate_part, grad_w_down), "dp")
    grad_mixed = dot_nt(grad_branch, w_out).astype(b16)
    grad_probs = dot_nt(grad_mixed, values)
    grad_capped = probs * (grad_probs - jnp.sum(probs * grad_probs, axis=-1, keepdims=True))
    grad_raw = (grad_capped * (1.0 - bent * bent)).astype(b16)
    grad_keys = dot_tn(grad_raw, queries)
    grad_values = dot_tn(probs_low, grad_mixed)
    kept = jnp.where(is_first, grad_keys, grad_values)
    sent = jnp.where(is_first, grad_values, grad_keys).astype(b16)
    sent = after(sent, grad_w_gate)
    grad_w_up = exchange(after(up_part, grad_w_gate), "dp")
    kept = kept + swapped(sent, "context", 1).astype(f32)
    kept = after(kept, grad_w_up)
    kept = kept.reshape(reach + 1, group, HEAD_SIZE)
    mine = kept[reach]
    for steps in range(1, reach + 1):
        mine = mine + shifted(kept[reach - steps].astype(b16), "dp", -steps).astype(f32)
    grad_queries = dot(grad_raw, keys)
    grad_query_pre = rotate_back(grad_queries, cosine_table, sine_table) * HEAD_SIZE ** (-0.5)
    grad_query_pre = grad_query_pre.astype(b16)
    grad_w_out = dot_tn(mixed, grad_branch)
    grad_w_out = jnp.swapaxes(grad_w_out.astype(b16).reshape(HEAD_SIZE, n, deep), 0, 1)
    grad_w_out = exchange(after(grad_w_out, mine), "dp")
    mine = jnp.where(is_first, rotate_back(mine, cosine_table, sine_table), mine).astype(b16)
    first_grad = dot_nt(grad_query_pre, query_in) + dot_nt(mine, pair_in)
    first_grad = collect_group(first_grad, sub)
    own_scale = rms_scale(own_tokens)
    own_normed = own_tokens * own_scale
    grad_inputs = grad_middle + rms_back(first_grad * gains[0], own_normed, own_scale)
    grad_inputs = spread_lanes(grad_inputs.astype(b16)).astype(f32)
    grad_gains = jnp.stack(
        [
            jnp.sum(first_grad * own_normed, axis=0),
            jnp.sum(grad_middle * normed_two, axis=0),
            jnp.sum(lifted_grad * normed_three, axis=0),
            jnp.sum(grad_out * normed_four, axis=0),
        ]
    )

    def row_blocks(right):
        return dot_tn(lifted_one, right).astype(b16).reshape(n, deep, HEAD_SIZE)

    grad_w_query = exchange(after(row_blocks(grad_query_pre), grad_w_out), "dp")
    rider = jnp.swapaxes(grad_gains.astype(b16).reshape(4, n, deep), 0, 1).reshape(n, -1)
    rider = jnp.pad(rider, ((0, 0), (0, 16 * HEAD_SIZE - rider.shape[1])))
    rider = jnp.concatenate([row_blocks(mine), rider.reshape(n, 16, HEAD_SIZE)], axis=1)
    grad_pair = summed(exchange(after(rider, grad_w_query), "dp"))
    grad_gains = grad_pair[deep:].reshape(-1)[: 4 * deep].reshape(4, 2, deep // 2)
    grad_gains, sent = picked(is_first, (grad_gains[:, 0], grad_gains[:, 1]))
    grad_gains = grad_gains + swapped(sent, "context", 1)
    grad_gains = grad_gains + swapped(grad_gains, "tensor", 2)
    grad_gains = grad_gains + swapped(grad_gains, "tensor", 1)

    def halves(total):
        kept, sent = picked(is_first, (total[: deep // 2], total[deep // 2 : deep]))
        return kept, swapped(sent.astype(b16), "context", 1).astype(f32)

    grad_w_query = jnp.concatenate(picked(is_first, halves(summed(grad_w_query))), axis=1)
    grad_w_key, grad_w_value = picked(is_first, halves(grad_pair))
    grad_w_out = summed(grad_w_out)
    kept = half_of(grad_w_out, side, 1)
    got = swapped(half_of(grad_w_out, 1 - side, 1).astype(b16), "context", 1).astype(f32)
    grad_w_out = jnp.concatenate(picked(is_first, (kept, got)), axis=0)

    grad_w_down = jnp.swapaxes(grad_w_down, 1, 2).reshape(n * units, deep // 2).astype(f32)
    grad_w_gate = jnp.swapaxes(grad_w_gate, 0, 1).reshape(deep // 2, n * units).astype(f32)
    grad_w_up = jnp.swapaxes(grad_w_up, 0, 1).reshape(deep // 2, n * units).astype(f32)
    return (
        output,
        grad_inputs,
        grad_w_query,
        grad_w_key,
        grad_w_value,
        grad_w_out,
        grad_w_gate,
        grad_w_up,
        grad_w_down,
        grad_gains[0],
        grad_gains[1],
        grad_gains[2],
        grad_gains[3],
    )


def solution(mesh):
    return jax.shard_map(
        on_device,
        mesh=mesh,
        in_specs=(
            P(("dp", "context"), None),
            P(("dp", "context")),
            P("dp", "tensor"),
            P("dp", "tensor"),
            P("dp", "tensor"),
            P("tensor", "dp"),
            P("dp", "tensor"),
            P("dp", "tensor"),
            P("tensor", "dp"),
            P("dp"),
            P("dp"),
            P("dp"),
            P("dp"),
            P(("dp", "context"), None),
        ),
        out_specs=(
            P(("dp", "context"), None),
            P(("dp", "context"), None),
            P(("dp", "context"), "tensor"),
            P(("dp", "context"), "tensor"),
            P(("dp", "context"), "tensor"),
            P("tensor", ("dp", "context")),
            P(("dp", "context"), "tensor"),
            P(("dp", "context"), "tensor"),
            P("tensor", ("dp", "context")),
            P(("dp", "context")),
            P(("dp", "context")),
            P(("dp", "context")),
            P(("dp", "context")),
        ),
        check_vma=False,
    )
```

```python
import jax
import jax.numpy as jnp
from jax import lax
from jax.experimental import pallas as pl
from jax.experimental.pallas import tpu as pltpu
from jax.sharding import PartitionSpec as P

HEAD_SIZE = 256
SLIDE_WINDOW = 4096


eps = 1e-06
softcap = 50.0
negative = -1e30
f32 = jnp.float32
b16 = jnp.bfloat16


def rms_scale(value_rows):
    return lax.rsqrt(jnp.mean(value_rows * value_rows, axis=-1, keepdims=True) + eps)


def rms_back(grad, normed, scale):
    return scale * (grad - normed * jnp.mean(grad * normed, axis=-1, keepdims=True))


def rotary_tables(positions):
    inverse = 1.0 / 10000.0 ** (jnp.arange(0, HEAD_SIZE, 2, dtype=f32) / HEAD_SIZE)
    angles = positions.astype(f32)[:, None] * inverse[None, :]
    return (jnp.cos(angles), jnp.sin(angles))


def apply_rotary(value_rows, cosine_table, sine_table):
    half = value_rows.shape[-1] // 2
    first, second = value_rows[:, :half], value_rows[:, half:]
    return jnp.concatenate(
        [first * cosine_table - second * sine_table, second * cosine_table + first * sine_table],
        axis=-1,
    )


def rotate_back(grads, cosine_table, sine_table):
    return apply_rotary(grads, cosine_table, -sine_table)


def gated(gate_value, up_value):
    return jax.nn.gelu(gate_value, approximate=True) * up_value


def exchange(blocks, axis):
    return lax.all_to_all(blocks, axis, 0, 0, tiled=True)


def gathered(block, axis):
    count = lax.axis_size(axis)
    return exchange(jnp.broadcast_to(block[None], (count,) + block.shape), axis)


def swapped(value, axis, bit):
    count = lax.axis_size(axis)
    return lax.ppermute(value, axis, [(place, place ^ bit) for place in range(count)])


def passed_on(value, steps, way):
    n = lax.axis_size("dp")
    pairs = [(s, s + 1) for s in range(steps - 1, n - 1)]
    if way < 0:
        pairs = [(n - 1 - s, n - 1 - t) for s, t in pairs]
    return lax.ppermute(value, "dp", pairs)


def shifted(value, axis, steps):
    count = lax.axis_size(axis)
    return lax.ppermute(
        value, axis, [(s, s + steps) for s in range(count) if 0 <= s + steps < count]
    )


def summed(blocks):
    return jnp.sum(blocks.astype(f32), axis=0)


def dot(left, right):
    return jnp.dot(left, right, preferred_element_type=f32)


def dot_nt(left, right):
    return lax.dot_general(left, right, (((1,), (1,)), ((), ())), preferred_element_type=f32)


def dot_tn(left, right):
    return lax.dot_general(left, right, (((0,), (0,)), ((), ())), preferred_element_type=f32)


def rotated(value, steps):
    n = lax.axis_size("dp")
    return lax.ppermute(value, "dp", [(s, (s + steps) % n) for s in range(n)])


def picked(first, pair):
    low, high = pair
    return jnp.where(first, low, high), jnp.where(first, high, low)


def after(value, *earlier):
    return lax.optimization_barrier((value,) + earlier)[0]


def ring_blocks(block):
    n = lax.axis_size("dp")
    return [block] + [rotated(block, steps) for steps in range(1, n)]


def in_order(blocks):
    n = lax.axis_size("dp")
    place = lax.axis_index("dp")
    blocks = [blocks[-j % n] for j in range(n)]
    for bit in range((n - 1).bit_length()):
        shift = 1 << bit
        odd = (place >> bit) % 2 == 1
        blocks = [jnp.where(odd, blocks[(j - shift) % n], blocks[j]) for j in range(n)]
    return jnp.stack(blocks)


def ring_summed(blocks):
    n = lax.axis_size("dp")
    place = lax.axis_index("dp")
    total = lax.dynamic_index_in_dim(blocks, place, 0, keepdims=False)
    for steps in range(1, n):
        sent = lax.dynamic_index_in_dim(blocks, (place + steps) % n, 0, keepdims=False)
        total = total + rotated(sent.astype(b16), steps).astype(f32)
    return total


def unit_blocks(weights, side, n):
    deep, total = weights[0].shape
    units = total // n
    shape = (n, deep // 2, units)
    if deep % 32:
        halves = [lax.dynamic_slice_in_dim(w, side * (deep // 2), deep // 2) for w in weights]
        return [jnp.swapaxes(w.reshape(deep // 2, n, units), 0, 1) for w in halves]

    def kernel(side_ref, *refs):
        for source, target in zip(refs[: len(weights)], refs[len(weights) :]):
            for j in range(n):
                target[j] = source[:, j * units : (j + 1) * units]

    return pl.pallas_call(
        kernel,
        grid_spec=pltpu.PrefetchScalarGridSpec(
            num_scalar_prefetch=1,
            grid=(1,),
            in_specs=[pl.BlockSpec((deep // 2, total), lambda g, s: (s[0], 0))] * len(weights),
            out_specs=[pl.BlockSpec(shape, lambda g, s: (0, 0, 0))] * len(weights),
        ),
        out_shape=[jax.ShapeDtypeStruct(shape, w.dtype) for w in weights],
        compiler_params=pltpu.CompilerParams(vmem_limit_bytes=48 << 20),
        name="unit_blocks",
    )(side.astype(jnp.int32).reshape(1), *weights)


def side_by_side(blocks):
    n, rows, units = blocks.shape
    if rows % 16:
        return jnp.swapaxes(blocks, 0, 1).reshape(rows, n * units).astype(f32)

    def kernel(source, target):
        for j in range(n):
            target[:, j * units : (j + 1) * units] = source[j].astype(f32)

    return pl.pallas_call(
        kernel,
        out_shape=jax.ShapeDtypeStruct((rows, n * units), f32),
        compiler_params=pltpu.CompilerParams(vmem_limit_bytes=32 << 20),
        name="side_by_side",
    )(blocks)


def bits():
    lane = lax.axis_index("tensor")
    return lax.axis_index("context") == 0, lane < 2, lane % 2 == 0


AXES = (("context", 1), ("tensor", 2), ("tensor", 1))


def join(own, step, axis):
    low, high = picked(bits()[step], (own, swapped(own, *AXES[step])))
    return jnp.stack([low, high], axis=axis)


def fold(partial, step, axis):
    low = lax.index_in_dim(partial, 0, axis, keepdims=False)
    high = lax.index_in_dim(partial, 1, axis, keepdims=False)
    kept, sent = picked(bits()[step], (low, high))
    return kept + swapped(sent.astype(b16), *AXES[step]).astype(f32)


def collect_group(partial, sub, *earlier):
    width = partial.shape[-1]
    partial = after(fold(partial.reshape(2, 2, 2, sub, width), 2, 2), *earlier)
    left, right = partial[..., : width // 2], partial[..., width // 2 :]
    left = fold(fold(left, 0, 0), 1, 0)
    right = fold(fold(right, 1, 1), 0, 0)
    return jnp.concatenate([left, right], axis=-1)


def spread_group(block, *earlier):
    width = block.shape[-1]
    left, right = block[:, : width // 2], block[:, width // 2 :]
    left = join(join(left, 0, 0), 1, 1)
    right = join(join(right, 1, 0), 0, 0)
    whole = after(jnp.concatenate([left, right], axis=-1), *earlier)
    whole = join(whole, 2, 2)
    return whole.reshape(-1, width)


def spread_lanes(block):
    return join(join(block, 1, 0), 2, 1).reshape(-1, block.shape[-1])


SMEM = pltpu.SMEM


def params(megabytes=48):
    return pltpu.CompilerParams(vmem_limit_bytes=megabytes << 20)


def scalar(value):
    return value.astype(jnp.int32).reshape(1)


def whole(shape):
    return pl.BlockSpec(shape, lambda *_: (0,) * len(shape))


def row_grad(left, right):
    width = left.shape[1]
    step = 384

    def kernel(left_ref, right_ref, out):
        for start in range(0, width, step):
            here = slice(start, start + step)
            out[here, :] = dot_tn(left_ref[:, here], right_ref[...]).astype(b16)

    return pl.pallas_call(
        kernel,
        out_shape=jax.ShapeDtypeStruct((width, right.shape[1]), b16),
        compiler_params=params(),
        name="row_grad",
    )(left, right)


def attend_back(rows, w_out, keys, values, queries, probs, bent, tables, side):
    group, width = rows.shape
    span, size = keys.shape
    block = 128
    steps = group // block

    def kernel(
        side_ref, rows_ref, out_ref, key_ref, value_ref, query_ref, probs_ref, bent_ref, cos_ref, sin_ref,
        query_grad, kept, sent, key_sum, value_sum,
    ):
        step = pl.program_id(0)
        mixed = dot(rows_ref[...], out_ref[...]).astype(b16)
        grads = dot_nt(mixed, value_ref[...])
        probs = probs_ref[...]
        bent = bent_ref[...]
        grads = probs * (grads - jnp.sum(probs * grads, axis=-1, keepdims=True))
        grads = (grads * (1.0 - bent * bent)).astype(b16)
        turned = rotate_back(dot(grads, key_ref[...]), cos_ref[...], sin_ref[...])
        query_grad[...] = (turned * HEAD_SIZE ** (-0.5)).astype(b16)
        key_part = dot_tn(grads, query_ref[...])
        value_part = dot_tn(probs.astype(b16), mixed)

        @pl.when(step == 0)
        def _():
            key_sum[...] = key_part
            value_sum[...] = value_part

        @pl.when(step > 0)
        def _():
            key_sum[...] += key_part
            value_sum[...] += value_part

        @pl.when((step == steps - 1) & (side_ref[0] == 0))
        def _():
            kept[...] = key_sum[...]
            sent[...] = value_sum[...].astype(b16)

        @pl.when((step == steps - 1) & (side_ref[0] == 1))
        def _():
            kept[...] = value_sum[...]
            sent[...] = key_sum[...].astype(b16)

    def by_rows(columns):
        return pl.BlockSpec((block, columns), lambda g: (g, 0))

    return pl.pallas_call(
        kernel,
        grid=(steps,),
        in_specs=[
            pl.BlockSpec(memory_space=SMEM),
            by_rows(width),
            whole((width, size)),
            whole((span, size)),
            whole((span, size)),
            by_rows(size),
            by_rows(span),
            by_rows(span),
            by_rows(size // 2),
            by_rows(size // 2),
        ],
        out_specs=[by_rows(size), whole((span, size)), whole((span, size))],
        out_shape=[
            jax.ShapeDtypeStruct((group, size), b16),
            jax.ShapeDtypeStruct((span, size), f32),
            jax.ShapeDtypeStruct((span, size), b16),
        ],
        scratch_shapes=[pltpu.VMEM((span, size), f32)] * 2,
        compiler_params=params(),
        name="attend_back",
    )(scalar(side), rows, w_out, keys, values, queries, probs, bent, *tables)


def together(*values):
    return lax.optimization_barrier(values)


def spread_chunk(block, *earlier):
    block = jnp.concatenate([block, swapped(block, "tensor", 2)], axis=0)
    block = after(block, *earlier)
    return jnp.concatenate([block, swapped(block, "tensor", 1)], axis=0)


def folded(partial, bit):
    half = partial.shape[0] // 2
    return partial[:half] + swapped(partial[half:].astype(b16), "tensor", bit).astype(f32)


def pipelined(block, work):
    n = lax.axis_size("dp")
    sub = block.shape[0]
    groups = [[0], [1, n - 1], list(range(2, n - 1))] if n > 3 else [[0], list(range(1, n))]
    rows, partial, rest = [], [], []
    sent = block
    for group in groups:
        got = [rotated(sent, steps) if steps else block for steps in group]
        if group[0]:
            sent = after(block, *got)
        rows.append(got)
    for number, got in enumerate(rows):
        got = jnp.concatenate(got, axis=0) if len(got) > 1 else got[0]
        rows[number] = spread_chunk(got, *partial[:1])
        first, *others = work(number, after(rows[number], *partial[-1:]))
        partial.append(first)
        rest.append(others)

    total = 0.0
    for number, group in enumerate(groups):
        back = folded(folded(partial[number], 1), 2)
        for place, steps in enumerate(group):
            part = back[place * sub : (place + 1) * sub]
            if steps:
                part = rotated(part.astype(b16), -steps).astype(f32)
            total = total + part
    return rows, total, list(zip(*rest)), partial + [back]


def on_device(
    tokens,
    segments,
    w_query,
    key_weight,
    value_weight,
    w_output,
    w_gate,
    w_up,
    w_down,
    pre_attn_gain,
    post_attn_gain,
    pre_ffw_gain,
    post_ffw_gain,
    cotangent,
):
    n = lax.axis_size("dp")
    place = lax.axis_index("dp")
    side = lax.axis_index("context")
    lane = lax.axis_index("tensor")
    lanes = lax.axis_size("tensor")
    rows, width = tokens.shape
    group = 2 * rows
    sub = rows // lanes
    deep = width // n
    reach = min((SLIDE_WINDOW + group - 2) // group, n - 1)
    is_first = side == 0

    def half_of(value, which, axis):
        size = value.shape[axis] // 2
        low = lax.slice_in_dim(value, 0, size, axis=axis)
        high = lax.slice_in_dim(value, size, 2 * size, axis=axis)
        return jnp.where(which == 0, low, high)

    def with_rider(block, values):
        rider = jnp.zeros((16 * HEAD_SIZE - values.size,), b16)
        rider = jnp.concatenate([values.astype(b16).reshape(-1), rider])
        return jnp.concatenate([block, rider.reshape(16, HEAD_SIZE)], axis=0)

    def split_rider(blocks, count):
        size = blocks.shape[1] - 16
        rider = blocks[:, size:].reshape(blocks.shape[0], -1)[:, :count]
        return blocks[:, :size], rider

    gains = jnp.concatenate([pre_attn_gain, post_attn_gain, pre_ffw_gain, post_ffw_gain])
    pair_got = ring_blocks(with_rider(jnp.where(is_first, key_weight, value_weight), gains))
    group_tokens = join(tokens, 0, 0).reshape(group, width).astype(f32)
    segment_pair = join(segments[None].astype(b16), 0, 0)
    pair_in, gains = split_rider(in_order(pair_got), 4 * deep)
    pair_in = pair_in.reshape(width, HEAD_SIZE)
    gains = 1.0 + jnp.swapaxes(gains.reshape(n, 4, deep), 0, 1).reshape(4, width).astype(f32)
    scale_one = rms_scale(group_tokens)
    normed_one = group_tokens * scale_one
    lifted_one = (normed_one * gains[0]).astype(b16)
    positions = place * group + jnp.arange(group, dtype=jnp.int32)
    cosine_table, sine_table = rotary_tables(positions)
    mine = dot(lifted_one, pair_in)
    mine = jnp.where(is_first, apply_rotary(mine, cosine_table, sine_table), mine).astype(b16)
    mine = [mine] + [shifted(mine, "dp", steps) for steps in range(1, reach + 1)]
    query_got = ring_blocks(after(with_rider(half_of(w_query, side, 1), segment_pair), mine[0]))
    query_in, all_segments = split_rider(in_order(query_got), group)
    query_in = query_in.reshape(width, HEAD_SIZE)
    all_segments = all_segments.reshape(-1).astype(jnp.int32)
    out_got = ring_blocks(after(half_of(w_output.T, side, 1), *query_got))
    w_out = in_order(out_got).reshape(width, HEAD_SIZE)

    units = w_gate.shape[1] // n
    gate_got, up_got, down_got = unit_blocks([w_gate, w_up, w_down.T], side, n)
    gate_got = exchange(after(gate_got, *mine), "dp")
    up_got = exchange(after(up_got, gate_got), "dp")
    down_got = exchange(after(down_got, up_got), "dp")
    gate_w = join(gate_got, 0, 1).reshape(width, units)
    up_w = join(up_got, 0, 1).reshape(width, units)
    down_w = join(down_got, 0, 1).reshape(width, units)

    theirs = [swapped(block, "context", 1) for block in mine]
    mine = jnp.concatenate(mine[::-1], axis=0)
    theirs = jnp.concatenate(theirs[::-1], axis=0)
    keys = jnp.where(is_first, mine, theirs)
    values = jnp.where(is_first, theirs, mine)
    queries = (
        apply_rotary(dot(lifted_one, query_in), cosine_table, sine_table) * HEAD_SIZE ** (-0.5)
    ).astype(b16)
    span = (reach + 1) * group
    key_positions = (place - reach) * group + jnp.arange(span, dtype=jnp.int32)
    padded = jnp.concatenate([jnp.full((reach * group,), -1, jnp.int32), all_segments])
    key_segments = lax.dynamic_slice_in_dim(padded, place * group, span)
    query_segments = key_segments[reach * group :]
    valid = (key_positions[None, :] <= positions[:, None]) & (
        positions[:, None] - key_positions[None, :] < SLIDE_WINDOW
    )
    valid = valid & (key_positions[None, :] >= 0)
    valid = valid & (key_segments[None, :] == query_segments[:, None])
    bent = jnp.tanh(dot_nt(queries, keys) / softcap)
    masked = jnp.where(valid, softcap * bent, negative)
    weights = jnp.exp(masked - jnp.max(masked, axis=-1, keepdims=True))
    probs = weights / jnp.sum(weights, axis=-1, keepdims=True)
    probs_low = probs.astype(b16)
    mixed = dot(after(probs_low, up_got, gate_w, *out_got), values).astype(b16)
    branch = collect_group(dot_nt(mixed, w_out), sub, up_w, down_got)

    own_tokens = lax.dynamic_slice_in_dim(tokens, lane * sub, sub).astype(f32)
    grad_out = lax.dynamic_slice_in_dim(cotangent, lane * sub, sub).astype(f32)
    scale_two = rms_scale(branch)
    normed_two = branch * scale_two
    middle = own_tokens + normed_two * gains[1]
    scale_three = rms_scale(middle)
    normed_three = middle * scale_three
    lifted_two = (normed_three * gains[2]).astype(b16)

    def feed(number, chunk):
        gate = dot(chunk, gate_w)
        upper = dot(chunk, up_w)
        hidden = gated(gate, upper).astype(b16)
        return dot_nt(hidden, down_w), gate, upper, hidden

    lifted_two, down, (gate, upper, hidden), unused = pipelined(lifted_two, feed)
    scale_four = rms_scale(down)
    normed_four = down * scale_four
    output = (middle + normed_four * gains[3]).astype(b16)

    def unit_grad(left, right):
        partial = dot_tn(jnp.concatenate(left, axis=0), jnp.concatenate(right, axis=0))
        return partial.reshape(n, 2, deep // 2, units)

    grad_down = rms_back(grad_out * gains[3], normed_four, scale_four).astype(b16)
    def feed_back(number, chunk):
        unused, pull = jax.vjp(gated, gate[number], upper[number])
        grad_gate, grad_upper = [side.astype(b16) for side in pull(dot(chunk, down_w))]
        partial = dot_nt(grad_gate, gate_w) + dot_nt(grad_upper, up_w)
        return partial, grad_gate, grad_upper

    grad_down, lifted_grad, (grad_gate, grad_upper), partial = pipelined(grad_down, feed_back)
    output = spread_lanes(after(output, *grad_down))
    down_sum = unit_grad(grad_down, after(hidden, partial[-3]))
    down_part = fold(down_sum, 0, 1).astype(b16)
    gate_sum = unit_grad(lifted_two, after(grad_gate, partial[-1]))
    gate_part = fold(after(gate_sum, down_part), 0, 1).astype(b16)
    up_sum = unit_grad(lifted_two, after(grad_upper, partial[-1]))
    up_part = fold(after(up_sum, gate_part), 0, 1).astype(b16)
    grad_w_down = exchange(down_part, "dp")
    lifted_grad = after(lifted_grad, down_part, gate_sum, up_sum)
    grad_middle = grad_out + rms_back(lifted_grad * gains[2], normed_three, scale_three)
    grad_branch = rms_back(grad_middle * gains[1], normed_two, scale_two).astype(b16)
    grad_w_gate = exchange(after(gate_part, grad_w_down), "dp")
    grad_branch = spread_group(after(grad_branch, output, grad_w_down, gate_part), grad_w_gate, up_part)

    def row_blocks(left, right):
        return row_grad(left, right).reshape(n, deep, HEAD_SIZE)

    grad_w_up = exchange(after(up_part, grad_w_gate), "dp")
    grad_w_out = ring_summed(after(row_blocks(grad_branch, mixed), grad_w_gate))
    grad_query_pre, kept, sent = attend_back(
        grad_branch, w_out, keys, values, queries, probs, bent, (cosine_table, sine_table), side
    )
    kept = kept.reshape(reach + 1, group, HEAD_SIZE)
    sent = sent.reshape(reach + 1, group, HEAD_SIZE)
    slots = [
        kept[slot] + swapped(sent[slot], "context", 1).astype(f32) for slot in range(reach + 1)
    ]
    slots[0] = after(slots[0], grad_w_up, grad_w_out)
    mine = slots[reach]
    for steps in range(reach, 0, -1):
        mine = mine + shifted(slots[reach - steps].astype(b16), "dp", -steps).astype(f32)
    grad_w_query = ring_summed(after(row_blocks(lifted_one, grad_query_pre), grad_w_out))
    mine = after(mine, grad_w_query)
    mine = jnp.where(is_first, rotate_back(mine, cosine_table, sine_table), mine).astype(b16)
    first_grad = dot_nt(grad_query_pre, query_in) + dot_nt(mine, pair_in)
    grad_gain_one = jnp.sum(first_grad * normed_one, axis=0)
    first_grad = collect_group(first_grad, sub)
    own_scale = rms_scale(own_tokens)
    own_normed = own_tokens * own_scale
    grad_inputs = grad_middle + rms_back(first_grad * gains[0], own_normed, own_scale)
    grad_inputs = grad_inputs.astype(b16)
    grad_gains = jnp.stack(
        [
            grad_gain_one,
            jnp.sum(grad_middle * normed_two, axis=0),
            jnp.sum(lifted_grad * normed_three, axis=0),
            jnp.sum(grad_out * normed_four, axis=0),
        ]
    )

    def halves(total):
        kept, sent = picked(is_first, (total[: deep // 2], total[deep // 2 : deep]))
        return kept, swapped(sent.astype(b16), "context", 1).astype(f32)

    rider = jnp.swapaxes(grad_gains.astype(b16).reshape(4, n, deep), 0, 1).reshape(n, -1)
    rider = jnp.pad(rider, ((0, 0), (0, 16 * HEAD_SIZE - rider.shape[1])))
    rider = jnp.concatenate([row_blocks(lifted_one, mine), rider.reshape(n, 16, HEAD_SIZE)], axis=1)
    grad_pair = ring_summed(rider)
    grad_inputs, grad_pair = together(grad_inputs, grad_pair)
    grad_inputs = spread_lanes(grad_inputs).astype(f32)
    grad_gains = grad_pair[deep:].reshape(-1)[: 4 * deep].reshape(4, 2, deep // 2)
    grad_gains, sent = picked(is_first, (grad_gains[:, 0], grad_gains[:, 1]))
    grad_gains = grad_gains + swapped(sent, "context", 1)
    grad_gains = grad_gains + swapped(grad_gains, "tensor", 2)
    grad_gains = grad_gains + swapped(grad_gains, "tensor", 1)
    grad_w_out = jnp.concatenate(picked(is_first, halves(grad_w_out)), axis=1).T
    grad_w_query = jnp.concatenate(picked(is_first, halves(grad_w_query)), axis=1)
    grad_w_key, grad_w_value = picked(is_first, halves(grad_pair))
    grad_w_down, grad_w_gate, grad_w_up = after(
        (grad_w_down, grad_w_gate, grad_w_up), grad_w_out
    )
    grad_w_down = side_by_side(grad_w_down).T
    grad_w_gate = side_by_side(grad_w_gate)
    grad_w_up = side_by_side(grad_w_up)
    return (
        output,
        grad_inputs,
        grad_w_query,
        grad_w_key,
        grad_w_value,
        grad_w_out,
        grad_w_gate,
        grad_w_up,
        grad_w_down,
        grad_gains[0],
        grad_gains[1],
        grad_gains[2],
        grad_gains[3],
    )


def solution(mesh):
    return jax.shard_map(
        on_device,
        mesh=mesh,
        in_specs=(
            P(("dp", "context"), None),
            P(("dp", "context")),
            P("dp", "tensor"),
            P("dp", "tensor"),
            P("dp", "tensor"),
            P("tensor", "dp"),
            P("dp", "tensor"),
            P("dp", "tensor"),
            P("tensor", "dp"),
            P("dp"),
            P("dp"),
            P("dp"),
            P("dp"),
            P(("dp", "context"), None),
        ),
        out_specs=(
            P(("dp", "context"), None),
            P(("dp", "context"), None),
            P(("dp", "context"), "tensor"),
            P(("dp", "context"), "tensor"),
            P(("dp", "context"), "tensor"),
            P("tensor", ("dp", "context")),
            P(("dp", "context"), "tensor"),
            P(("dp", "context"), "tensor"),
            P("tensor", ("dp", "context")),
            P(("dp", "context")),
            P(("dp", "context")),
            P(("dp", "context")),
            P(("dp", "context")),
        ),
        check_vma=False,
    )
```

```python
import math

import jax
import jax.numpy as jnp
from jax import lax
from jax.experimental import pallas as pl
from jax.experimental.pallas import tpu as pltpu
from jax.sharding import PartitionSpec as P

HEAD_SIZE = 256
SLIDE_WINDOW = 4096


eps = 1e-06
softcap = 50.0
negative = -1e30
f32 = jnp.float32
b16 = jnp.bfloat16


def rms_scale(value_rows):
    return lax.rsqrt(jnp.mean(value_rows * value_rows, axis=-1, keepdims=True) + eps)


def rms_back(grad, normed, scale):
    return scale * (grad - normed * jnp.mean(grad * normed, axis=-1, keepdims=True))


def rotary_tables(positions):
    inverse = 1.0 / 10000.0 ** (jnp.arange(0, HEAD_SIZE, 2, dtype=f32) / HEAD_SIZE)
    angles = positions.astype(f32)[:, None] * inverse[None, :]
    return (jnp.cos(angles), jnp.sin(angles))


def apply_rotary(value_rows, cosine_table, sine_table):
    half = value_rows.shape[-1] // 2
    first, second = value_rows[:, :half], value_rows[:, half:]
    return jnp.concatenate(
        [first * cosine_table - second * sine_table, second * cosine_table + first * sine_table],
        axis=-1,
    )


def rotate_back(grads, cosine_table, sine_table):
    return apply_rotary(grads, cosine_table, -sine_table)


def gated(gate_value, up_value):
    return jax.nn.gelu(gate_value, approximate=True) * up_value


def exchange(blocks, axis):
    return lax.all_to_all(blocks, axis, 0, 0, tiled=True)


def gathered(block, axis):
    count = lax.axis_size(axis)
    return exchange(jnp.broadcast_to(block[None], (count,) + block.shape), axis)


def swapped(value, axis, bit):
    count = lax.axis_size(axis)
    return lax.ppermute(value, axis, [(place, place ^ bit) for place in range(count)])


def passed_on(value, steps, way):
    n = lax.axis_size("dp")
    pairs = [(s, s + 1) for s in range(steps - 1, n - 1)]
    if way < 0:
        pairs = [(n - 1 - s, n - 1 - t) for s, t in pairs]
    return lax.ppermute(value, "dp", pairs)


def shifted(value, axis, steps):
    count = lax.axis_size(axis)
    return lax.ppermute(
        value, axis, [(s, s + steps) for s in range(count) if 0 <= s + steps < count]
    )


def summed(blocks):
    return jnp.sum(blocks.astype(f32), axis=0)


def dot(left, right):
    return jnp.dot(left, right, preferred_element_type=f32)


def dot_nt(left, right):
    return lax.dot_general(left, right, (((1,), (1,)), ((), ())), preferred_element_type=f32)


def dot_tn(left, right):
    return lax.dot_general(left, right, (((0,), (0,)), ((), ())), preferred_element_type=f32)


def rotated(value, steps):
    n = lax.axis_size("dp")
    return lax.ppermute(value, "dp", [(s, (s + steps) % n) for s in range(n)])


def picked(first, pair):
    low, high = pair
    return jnp.where(first, low, high), jnp.where(first, high, low)


def after(value, *earlier):
    return lax.optimization_barrier((value,) + earlier)[0]


def ring_blocks(block):
    n = lax.axis_size("dp")
    return [block] + [rotated(block, steps) for steps in range(1, n)]


def in_order(blocks):
    n = lax.axis_size("dp")
    place = lax.axis_index("dp")
    blocks = [blocks[-j % n] for j in range(n)]
    for bit in range((n - 1).bit_length()):
        shift = 1 << bit
        odd = (place >> bit) % 2 == 1
        blocks = [jnp.where(odd, blocks[(j - shift) % n], blocks[j]) for j in range(n)]
    return jnp.stack(blocks)


def ring_summed(blocks, *earlier):
    n = lax.axis_size("dp")
    place = lax.axis_index("dp")
    total = lax.dynamic_index_in_dim(blocks, place, 0, keepdims=False).astype(f32)
    got = [
        rotated(
            lax.dynamic_index_in_dim(blocks, (place + steps) % n, 0, keepdims=False), steps
        )
        for steps in range(1, n)
    ]
    got = after(got, *earlier)
    for block in got:
        total = total + block.astype(f32)
    return total


def unit_blocks(weights, side, n):
    deep, total = weights[0].shape
    units = total // n
    shape = (n, deep // 2, units)
    if deep % 32:
        halves = [lax.dynamic_slice_in_dim(w, side * (deep // 2), deep // 2) for w in weights]
        return [jnp.swapaxes(w.reshape(deep // 2, n, units), 0, 1) for w in halves]

    def kernel(side_ref, *refs):
        for source, target in zip(refs[: len(weights)], refs[len(weights) :]):
            for j in range(n):
                target[j] = source[:, j * units : (j + 1) * units]

    return pl.pallas_call(
        kernel,
        grid_spec=pltpu.PrefetchScalarGridSpec(
            num_scalar_prefetch=1,
            grid=(1,),
            in_specs=[pl.BlockSpec((deep // 2, total), lambda g, s: (s[0], 0))] * len(weights),
            out_specs=[pl.BlockSpec(shape, lambda g, s: (0, 0, 0))] * len(weights),
        ),
        out_shape=[jax.ShapeDtypeStruct(shape, w.dtype) for w in weights],
        compiler_params=pltpu.CompilerParams(vmem_limit_bytes=48 << 20),
        name="unit_blocks",
    )(side.astype(jnp.int32).reshape(1), *weights)


def side_by_side(blocks):
    n, rows, units = blocks.shape
    if rows % 16:
        return jnp.swapaxes(blocks, 0, 1).reshape(rows, n * units).astype(f32)

    def kernel(source, target):
        for j in range(n):
            target[:, j * units : (j + 1) * units] = source[j].astype(f32)

    return pl.pallas_call(
        kernel,
        out_shape=jax.ShapeDtypeStruct((rows, n * units), f32),
        compiler_params=params(16),
        name="side_by_side",
    )(blocks)


def bits():
    lane = lax.axis_index("tensor")
    return lax.axis_index("context") == 0, lane < 2, lane % 2 == 0


AXES = (("context", 1), ("tensor", 2), ("tensor", 1))


def join(own, step, axis):
    low, high = picked(bits()[step], (own, swapped(own, *AXES[step])))
    return jnp.stack([low, high], axis=axis)


def fold(partial, step, axis):
    low = lax.index_in_dim(partial, 0, axis, keepdims=False)
    high = lax.index_in_dim(partial, 1, axis, keepdims=False)
    kept, sent = picked(bits()[step], (low, high))
    return kept + swapped(sent.astype(b16), *AXES[step]).astype(f32)


def half_sent(partial, step, axis):
    low = lax.index_in_dim(partial, 0, axis, keepdims=False)
    high = lax.index_in_dim(partial, 1, axis, keepdims=False)
    kept, sent = picked(bits()[step], (low, high))
    return kept, swapped(sent.astype(b16), *AXES[step])


def collect_group(partial, sub, *earlier):
    width = partial.shape[-1]
    partial = after(fold(partial.reshape(2, 2, 2, sub, width), 2, 2), *earlier)
    left, right = partial[..., : width // 2], partial[..., width // 2 :]
    left = fold(fold(left, 0, 0), 1, 0)
    right = fold(fold(right, 1, 1), 0, 0)
    return jnp.concatenate([left, right], axis=-1)


SMEM = pltpu.SMEM
VMEM = pltpu.VMEM


def params(megabytes=48):
    return pltpu.CompilerParams(vmem_limit_bytes=megabytes << 20)


def scalar(value):
    return value.astype(jnp.int32).reshape(1)


def whole(shape):
    return pl.BlockSpec(shape, lambda *_: (0,) * len(shape))


def fused(function, flags, *args):
    shapes = jax.eval_shape(function, *flags, *args)
    leaves, tree = jax.tree.flatten(shapes)
    size = sum(math.prod(v.shape) * v.dtype.itemsize for v in (*args, *leaves))
    if size > 32 << 20:
        return function(*flags, *args)
    count = len(flags)

    def kernel(*refs):
        given = [ref[0] == 1 for ref in refs[:count]]
        given += [ref[...] for ref in refs[count : count + len(args)]]
        results = jax.tree.leaves(function(*given))
        for ref, result in zip(refs[count + len(args) :], results):
            ref[...] = result

    out = pl.pallas_call(
        kernel,
        in_specs=[pl.BlockSpec(memory_space=SMEM)] * count
        + [pl.BlockSpec(memory_space=VMEM)] * len(args),
        out_specs=[pl.BlockSpec(memory_space=VMEM)] * len(leaves),
        out_shape=leaves,
        compiler_params=params(8 + (size >> 20)),
        name="fused_" + getattr(function, "__name__", "part").strip("<>_"),
    )(*[scalar(flag) for flag in flags], *args)
    return jax.tree.unflatten(tree, out)


def join_kernel(own, step, axis):
    other = swapped(own, *AXES[step])
    first = bits()[step]
    if own.ndim < 2 or own.shape[-2] % 16:
        return jnp.stack(picked(first, (own, other)), axis=axis)
    shape = own.shape[:axis] + (2,) + own.shape[axis:]

    def kernel(place, own_ref, other_ref, out):
        lead = (slice(None),) * axis
        out[(*lead, place[0])] = own_ref[...]
        out[(*lead, 1 - place[0])] = other_ref[...]

    return pl.pallas_call(
        kernel,
        in_specs=[pl.BlockSpec(memory_space=SMEM)] + [pl.BlockSpec(memory_space=VMEM)] * 2,
        out_specs=pl.BlockSpec(memory_space=VMEM),
        out_shape=jax.ShapeDtypeStruct(shape, own.dtype),
        compiler_params=params(8),
        name="join",
    )(1 - scalar(first), own, other)


def parted(first, low, high):
    kept, sent = picked(first, (low, high))
    return kept, sent.astype(b16)


def core_parted(low_core, out, sub):
    parts = [out[k * sub : (k + 1) * sub] for k in range(8)]
    pairs = [parted(low_core, parts[2 * k], parts[2 * k + 1]) for k in range(4)]
    return tuple(
        jnp.concatenate([pair[which] for pair in pairs], axis=0).reshape(2, 2, sub, -1)
        for which in range(2)
    )


def collect_halves(kept, sent, *earlier):
    half = kept.shape[-1] // 2
    context, high, low = bits()

    def halve(context, high, kept, got):
        total = kept + got.astype(f32)
        left, right = total[..., :half], total[..., half:]
        left = parted(context, left[0], left[1])
        right = parted(high, right[:, 0], right[:, 1])
        return *left, *right

    def again(context, high, left, left_got, right, right_got):
        left = left + left_got.astype(f32)
        right = right + right_got.astype(f32)
        return *parted(high, left[0], left[1]), *parted(context, right[0], right[1])

    got = swapped(sent, *AXES[2])
    left, left_sent, right, right_sent = fused(halve, (context, high), kept, got)
    left_sent, right_sent = after((left_sent, right_sent), *earlier)
    left_got, right_got = swapped(left_sent, *AXES[0]), swapped(right_sent, *AXES[1])
    left, left_sent, right, right_sent = fused(
        again, (context, high), left, left_got, right, right_got
    )
    return left, swapped(left_sent, *AXES[1]), right, swapped(right_sent, *AXES[0])


def halves_summed(left, left_got, right, right_got):
    return jnp.concatenate([left + left_got.astype(f32), right + right_got.astype(f32)], axis=-1)


def side_by_side_columns(left, right):
    return jnp.concatenate([left, right], axis=-1)


def spread_group(block):
    width = block.shape[-1]
    left, right = block[:, : width // 2], block[:, width // 2 :]
    left = join_kernel(join_kernel(left, 0, 0), 1, 1)
    right = join_kernel(join_kernel(right, 1, 0), 0, 0)
    return join_kernel(fused(side_by_side_columns, (), left, right), 2, 2).reshape(-1, width)


def spread_lanes(block):
    return join_kernel(join_kernel(block, 1, 0), 2, 1).reshape(-1, block.shape[-1])


def row_grad(left, right):
    width = left.shape[1]
    step = 384

    def kernel(left_ref, right_ref, out):
        for start in range(0, width, step):
            here = slice(start, start + step)
            out[here, :] = dot_tn(left_ref[:, here], right_ref[...]).astype(b16)

    return pl.pallas_call(
        kernel,
        out_shape=jax.ShapeDtypeStruct((width, right.shape[1]), b16),
        compiler_params=params(16),
        name="row_grad",
    )(left, right)


def attend_back(rows, w_out, keys, values, queries, probs, bent, tables, side):
    group, width = rows.shape
    span, size = keys.shape
    block = 128
    steps = group // block

    def kernel(
        side_ref, rows_ref, out_ref, key_ref, value_ref, query_ref, probs_ref, bent_ref, cos_ref, sin_ref,
        query_grad, kept, sent, key_sum, value_sum,
    ):
        step = pl.program_id(0)
        mixed = dot(rows_ref[...], out_ref[...]).astype(b16)
        grads = dot_nt(mixed, value_ref[...])
        probs = probs_ref[...]
        bent = bent_ref[...]
        grads = probs * (grads - jnp.sum(probs * grads, axis=-1, keepdims=True))
        grads = (grads * (1.0 - bent * bent)).astype(b16)
        turned = rotate_back(dot(grads, key_ref[...]), cos_ref[...], sin_ref[...])
        query_grad[...] = (turned * HEAD_SIZE ** (-0.5)).astype(b16)
        key_part = dot_tn(grads, query_ref[...])
        value_part = dot_tn(probs.astype(b16), mixed)

        @pl.when(step == 0)
        def _():
            key_sum[...] = key_part
            value_sum[...] = value_part

        @pl.when(step > 0)
        def _():
            key_sum[...] += key_part
            value_sum[...] += value_part

        @pl.when((step == steps - 1) & (side_ref[0] == 0))
        def _():
            kept[...] = key_sum[...]
            sent[...] = value_sum[...].astype(b16)

        @pl.when((step == steps - 1) & (side_ref[0] == 1))
        def _():
            kept[...] = value_sum[...]
            sent[...] = key_sum[...].astype(b16)

    def by_rows(columns):
        return pl.BlockSpec((block, columns), lambda g: (g, 0))

    return pl.pallas_call(
        kernel,
        grid=(steps,),
        in_specs=[
            pl.BlockSpec(memory_space=SMEM),
            by_rows(width),
            whole((width, size)),
            whole((span, size)),
            whole((span, size)),
            by_rows(size),
            by_rows(span),
            by_rows(span),
            by_rows(size // 2),
            by_rows(size // 2),
        ],
        out_specs=[by_rows(size), whole((span, size)), whole((span, size))],
        out_shape=[
            jax.ShapeDtypeStruct((group, size), b16),
            jax.ShapeDtypeStruct((span, size), f32),
            jax.ShapeDtypeStruct((span, size), b16),
        ],
        scratch_shapes=[pltpu.VMEM((span, size), f32)] * 2,
        compiler_params=params(),
        name="attend_back",
    )(scalar(side), rows, w_out, keys, values, queries, probs, bent, *tables)


def together(*values):
    return lax.optimization_barrier(values)


def added(terms):
    total = terms[0].astype(f32)
    for term in terms[1:]:
        total = total + term.astype(f32)
    return total


def spread_chunk(block, *earlier):
    block = jnp.concatenate([block, swapped(block, "tensor", 2)], axis=0)
    block = after(block, *earlier)
    return jnp.concatenate([block, swapped(block, "tensor", 1)], axis=0)


def folded(partial, bit):
    half = partial.shape[0] // 2
    return partial[:half] + swapped(partial[half:].astype(b16), "tensor", bit).astype(f32)


def pipelined(block, work):
    n = lax.axis_size("dp")
    sub = block.shape[0]
    groups = [[0], [1, n - 1], list(range(2, n - 1))] if n > 3 else [[0], list(range(1, n))]
    rows, partial, rest = [], [], []
    sent = block
    for group in groups:
        got = [rotated(sent, steps) if steps else block for steps in group]
        if group[0]:
            sent = after(block, *got)
        rows.append(got)
    near = rows[1]
    for number, got in enumerate(rows):
        got = jnp.concatenate(got, axis=0) if len(got) > 1 else got[0]
        rows[number] = spread_chunk(got, *partial[:1])
        first, *others = work(number, after(rows[number], *partial[-1:]), *near)
        partial.append(first)
        rest.append(others)

    terms, earlier = [], []
    for number in list(range(1, len(groups))) + [0]:
        back = after(folded(partial[number], 1), *earlier)
        back = folded(back, 2)
        earlier = [back]
        for place, steps in enumerate(groups[number]):
            part = back[place * sub : (place + 1) * sub]
            terms.append(rotated(part.astype(b16), -steps) if steps else part)
    return rows, terms, list(zip(*rest)), partial + earlier


def on_device(
    tokens,
    segments,
    w_query,
    key_weight,
    value_weight,
    w_output,
    w_gate,
    w_up,
    w_down,
    pre_attn_gain,
    post_attn_gain,
    pre_ffw_gain,
    post_ffw_gain,
    cotangent,
):
    n = lax.axis_size("dp")
    place = lax.axis_index("dp")
    side = lax.axis_index("context")
    lane = lax.axis_index("tensor")
    lanes = lax.axis_size("tensor")
    rows, width = tokens.shape
    group = 2 * rows
    sub = rows // lanes
    deep = width // n
    reach = min((SLIDE_WINDOW + group - 2) // group, n - 1)
    is_first = side == 0

    def half_of(value, which, axis):
        size = value.shape[axis] // 2
        low = lax.slice_in_dim(value, 0, size, axis=axis)
        high = lax.slice_in_dim(value, size, 2 * size, axis=axis)
        return jnp.where(which == 0, low, high)

    def with_rider(block, values):
        rider = jnp.zeros((16 * HEAD_SIZE - values.size,), b16)
        rider = jnp.concatenate([values.astype(b16).reshape(-1), rider])
        return jnp.concatenate([block, rider.reshape(16, HEAD_SIZE)], axis=0)

    def split_rider(blocks, count):
        size = blocks.shape[1] - 16
        rider = blocks[:, size:].reshape(blocks.shape[0], -1)[:, :count]
        return blocks[:, :size], rider

    gains = jnp.concatenate([pre_attn_gain, post_attn_gain, pre_ffw_gain, post_ffw_gain])
    pair_got = ring_blocks(with_rider(jnp.where(is_first, key_weight, value_weight), gains))
    group_tokens = join(tokens, 0, 0).reshape(group, width)
    segment_pair = join(segments[None].astype(b16), 0, 0)
    pair_in, gains = split_rider(in_order(pair_got), 4 * deep)
    pair_in = pair_in.reshape(width, HEAD_SIZE)
    gains = 1.0 + jnp.swapaxes(gains.reshape(n, 4, deep), 0, 1).reshape(4, width).astype(f32)
    normed_one = group_tokens.astype(f32)
    normed_one = normed_one * rms_scale(normed_one)
    lifted_one = (normed_one * gains[0]).astype(b16)
    positions = place * group + jnp.arange(group, dtype=jnp.int32)
    cosine_table, sine_table = rotary_tables(positions)
    mine = dot(lifted_one, pair_in)
    mine = jnp.where(is_first, apply_rotary(mine, cosine_table, sine_table), mine).astype(b16)
    mine = [mine] + [shifted(mine, "dp", steps) for steps in range(1, reach + 1)]
    query_got = ring_blocks(after(with_rider(half_of(w_query, side, 1), segment_pair), mine[0]))
    query_in, all_segments = split_rider(in_order(query_got), group)
    query_in = query_in.reshape(width, HEAD_SIZE)
    all_segments = all_segments.reshape(-1).astype(jnp.int32)
    out_got = ring_blocks(after(half_of(w_output.T, side, 1), *query_got))
    w_out = in_order(out_got).reshape(width, HEAD_SIZE)

    units = w_gate.shape[1] // n
    gate_got, up_got, down_got = unit_blocks([w_gate, w_up, w_down.T], side, n)
    gate_got = exchange(after(gate_got, *mine), "dp")
    up_got = exchange(after(up_got, gate_got), "dp")
    down_got = exchange(after(down_got, up_got), "dp")
    gate_other, up_other, down_other = [
        swapped(got, "context", 1) for got in (gate_got, up_got, down_got)
    ]

    def both_halves(own, other):
        return jnp.stack(picked(is_first, (own, other)), axis=1).reshape(width, units)

    theirs = [swapped(block, "context", 1) for block in mine]
    mine = jnp.concatenate(mine[::-1], axis=0)
    theirs = jnp.concatenate(theirs[::-1], axis=0)
    keys = jnp.where(is_first, mine, theirs)
    values = jnp.where(is_first, theirs, mine)
    queries = (
        apply_rotary(dot(lifted_one, query_in), cosine_table, sine_table) * HEAD_SIZE ** (-0.5)
    ).astype(b16)
    span = (reach + 1) * group
    key_positions = (place - reach) * group + jnp.arange(span, dtype=jnp.int32)
    padded = jnp.concatenate([jnp.full((reach * group,), -1, jnp.int32), all_segments])
    key_segments = lax.dynamic_slice_in_dim(padded, place * group, span)
    query_segments = key_segments[reach * group :]
    valid = (key_positions[None, :] <= positions[:, None]) & (
        positions[:, None] - key_positions[None, :] < SLIDE_WINDOW
    )
    valid = valid & (key_positions[None, :] >= 0)
    valid = valid & (key_segments[None, :] == query_segments[:, None])
    bent = jnp.tanh(dot_nt(queries, keys) / softcap)
    masked = jnp.where(valid, softcap * bent, negative)
    weights = jnp.exp(masked - jnp.max(masked, axis=-1, keepdims=True))
    probs = weights / jnp.sum(weights, axis=-1, keepdims=True)
    probs_low = probs.astype(b16)
    mixed = dot(after(probs_low, gate_got, *out_got), values).astype(b16)
    branch = after(collect_group(dot_nt(mixed, w_out), sub), up_got)

    own_tokens = lax.dynamic_slice_in_dim(tokens, lane * sub, sub)
    own_cotangent = lax.dynamic_slice_in_dim(cotangent, lane * sub, sub)
    grad_out = own_cotangent.astype(f32)
    scale_two = rms_scale(branch)
    normed_two = branch * scale_two
    middle = own_tokens.astype(f32) + normed_two * gains[1]
    scale_three = rms_scale(middle)
    normed_three = middle * scale_three
    lifted_two = after((normed_three * gains[2]).astype(b16), down_got)
    gate_w = both_halves(gate_got, after(gate_other, lifted_two))
    up_w = both_halves(up_got, after(up_other, lifted_two))

    def feed(number, chunk, *arrived):
        down_w = both_halves(down_got, after(down_other, *arrived))
        gate = dot(chunk, gate_w)
        upper = dot(chunk, up_w)
        hidden = gated(gate, upper).astype(b16)
        return dot_nt(hidden, down_w), gate, upper, hidden

    lifted_two, terms, (gate, upper, hidden), unused = pipelined(lifted_two, feed)
    down = added(terms)
    scale_four = rms_scale(down)
    normed_four = down * scale_four
    output = (middle + normed_four * gains[3]).astype(b16)

    grad_gain_four = jnp.sum(grad_out * normed_four, axis=0, keepdims=True)
    def unit_grad(left, right):
        partial = dot_tn(jnp.concatenate(left, axis=0), jnp.concatenate(right, axis=0))
        return partial.reshape(n, 2, deep // 2, units)

    grad_down = rms_back(grad_out * gains[3], normed_four, scale_four).astype(b16)
    down_w = both_halves(down_got, down_other)

    def feed_back(number, chunk, *arrived):
        unused, pull = jax.vjp(gated, gate[number], upper[number])
        grad_gate, grad_upper = [side.astype(b16) for side in pull(dot(chunk, down_w))]
        partial = dot_nt(grad_gate, gate_w) + dot_nt(grad_upper, up_w)
        return partial, grad_gate, grad_upper

    grad_down, terms, (grad_gate, grad_upper), partial = pipelined(grad_down, feed_back)
    output = spread_lanes(after(output, *grad_down))
    down_sum = unit_grad(grad_down, after(hidden, partial[-3]))
    down_kept, down_got = half_sent(down_sum, 0, 1)
    gate_sum = unit_grad(lifted_two, after(grad_gate, partial[-1]))
    up_sum = unit_grad(lifted_two, after(grad_upper, partial[-1]))
    terms, down_got, gate_sum, up_sum = together(terms, down_got, gate_sum, up_sum)

    def two_sided(kept, got):
        return (kept + got.astype(f32)).astype(b16)

    def middle_back(cotangent, gains, scale_two, normed_two, scale_three, normed_three, *terms):
        grad_out = cotangent.astype(f32)
        lifted_grad = added(terms)
        grad_middle = grad_out + rms_back(lifted_grad * gains[2:3], normed_three, scale_three)
        grad_branch = rms_back(grad_middle * gains[1:2], normed_two, scale_two).astype(b16)
        gain_two = jnp.sum(grad_middle * normed_two, axis=0, keepdims=True)
        gain_three = jnp.sum(lifted_grad * normed_three, axis=0, keepdims=True)
        return grad_middle, grad_branch, gain_two, gain_three

    down_part = (down_kept + down_got.astype(f32)).astype(b16)
    grad_w_down = exchange(down_part, "dp")
    gate_kept, gate_got = half_sent(gate_sum, 0, 1)
    grad_middle, grad_branch, grad_gain_two, grad_gain_three = fused(
        middle_back, (), own_cotangent, gains, scale_two, normed_two, scale_three, normed_three, *terms
    )
    grad_branch, grad_w_down, gate_got = together(grad_branch, grad_w_down, gate_got)
    gate_part = (gate_kept + gate_got.astype(f32)).astype(b16)

    low_core = bits()[2]

    def row_blocks(left, right):
        return row_grad(left, right).reshape(n, deep, HEAD_SIZE)

    grad_w_gate = exchange(gate_part, "dp")
    up_kept, up_got = half_sent(up_sum, 0, 1)
    grad_branch = spread_group(grad_branch)
    out_blocks = row_blocks(grad_branch, mixed)
    grad_query_pre, kept, sent = attend_back(
        grad_branch, w_out, keys, values, queries, probs, bent, (cosine_table, sine_table), side
    )
    query_blocks = row_blocks(lifted_one, grad_query_pre)
    up_got, kept = together(up_got, kept)
    up_part = (up_kept + up_got.astype(f32)).astype(b16)
    grad_w_up = exchange(after(up_part, grad_w_gate), "dp")
    kept, sent, out_blocks, query_blocks, output = together(
        kept, sent, after(out_blocks, grad_w_gate), query_blocks, output
    )
    kept = kept.reshape(reach + 1, group, HEAD_SIZE)
    sent = sent.reshape(reach + 1, group, HEAD_SIZE)

    def full(kept, got):
        return kept + got.astype(f32)

    slots = [
        fused(two_sided if slot < reach else full, (), kept[slot], swapped(sent[slot], "context", 1))
        for slot in range(reach + 1)
    ]
    grad_w_out = ring_summed(out_blocks)
    terms = [slots[reach]]
    for steps in range(reach, 0, -1):
        terms.append(shifted(slots[reach - steps], "dp", -steps))
    terms, grad_w_up, grad_w_out = together(terms, grad_w_up, grad_w_out)

    def unturned(is_first, cosine, sine, *terms):
        total = added(terms)
        return jnp.where(is_first, rotate_back(total, cosine, sine), total).astype(b16)

    mine = fused(unturned, (is_first,), cosine_table, sine_table, *terms)
    pair_blocks = row_blocks(lifted_one, mine)

    def first_product(low_core, tokens, query_grad, query_in, pair_grad, pair_in):
        out = dot_nt(query_grad, query_in) + dot_nt(pair_grad, pair_in)
        values = tokens.astype(f32)
        gain = jnp.sum(out * (values * rms_scale(values)), axis=0, keepdims=True)
        return *core_parted(low_core, out, sub), gain

    kept, sent, grad_gain_one = fused(
        first_product,
        (low_core,),
        group_tokens,
        grad_query_pre,
        query_in,
        after(mine, pair_blocks),
        pair_in,
    )
    first_grad = collect_halves(kept, sent)

    def first_back(own_tokens, gains, grad_middle, *halves):
        first_grad = halves_summed(*halves)
        values = own_tokens.astype(f32)
        scale = rms_scale(values)
        return (grad_middle + rms_back(first_grad * gains[:1], values * scale, scale)).astype(b16)

    grad_inputs = fused(first_back, (), own_tokens, gains, grad_middle, *first_grad)
    grad_gains = jnp.concatenate(
        [grad_gain_one, grad_gain_two, grad_gain_three, grad_gain_four], axis=0
    )

    def halves(total):
        kept, sent = picked(is_first, (total[: deep // 2], total[deep // 2 : deep]))
        return kept, swapped(sent.astype(b16), "context", 1).astype(f32)

    grad_w_query = ring_summed(after(query_blocks, *terms), grad_inputs)
    grad_pair = ring_summed(pair_blocks, grad_inputs)
    grad_gains = after(grad_gains, grad_inputs)
    grad_gains = grad_gains + swapped(grad_gains, "tensor", 2)
    grad_gains = grad_gains + swapped(grad_gains, "tensor", 1)
    grad_gains = jnp.transpose(grad_gains.reshape(4, n, 2, deep // 2), (2, 1, 0, 3))
    grad_gains, sent = picked(is_first, (grad_gains[0], grad_gains[1]))
    grad_gains = ring_summed(grad_gains + swapped(sent, "context", 1))
    grad_inputs = spread_lanes(grad_inputs).astype(f32)
    grad_w_out = jnp.concatenate(picked(is_first, halves(grad_w_out)), axis=1).T
    grad_w_query = jnp.concatenate(picked(is_first, halves(grad_w_query)), axis=1)
    grad_w_key, grad_w_value = picked(is_first, halves(grad_pair))
    grad_w_down, grad_w_gate, grad_w_up = after(
        (grad_w_down, grad_w_gate, grad_w_up), mine
    )
    grad_w_down = side_by_side(grad_w_down).T
    grad_w_gate = side_by_side(grad_w_gate)
    grad_w_up = side_by_side(grad_w_up)
    return (
        output,
        grad_inputs,
        grad_w_query,
        grad_w_key,
        grad_w_value,
        grad_w_out,
        grad_w_gate,
        grad_w_up,
        grad_w_down,
        grad_gains[0],
        grad_gains[1],
        grad_gains[2],
        grad_gains[3],
    )


def solution(mesh):
    return jax.shard_map(
        on_device,
        mesh=mesh,
        in_specs=(
            P(("dp", "context"), None),
            P(("dp", "context")),
            P("dp", "tensor"),
            P("dp", "tensor"),
            P("dp", "tensor"),
            P("tensor", "dp"),
            P("dp", "tensor"),
            P("dp", "tensor"),
            P("tensor", "dp"),
            P("dp"),
            P("dp"),
            P("dp"),
            P("dp"),
            P(("dp", "context"), None),
        ),
        out_specs=(
            P(("dp", "context"), None),
            P(("dp", "context"), None),
            P(("dp", "context"), "tensor"),
            P(("dp", "context"), "tensor"),
            P(("dp", "context"), "tensor"),
            P("tensor", ("dp", "context")),
            P(("dp", "context"), "tensor"),
            P(("dp", "context"), "tensor"),
            P("tensor", ("dp", "context")),
            P(("dp", "context")),
            P(("dp", "context")),
            P(("dp", "context")),
            P(("dp", "context")),
        ),
        check_vma=False,
    )
```

```python
import math

import jax
import jax.numpy as jnp
from jax import lax
from jax.experimental import pallas as pl
from jax.experimental.pallas import tpu as pltpu
from jax.sharding import PartitionSpec as P

HEAD_SIZE = 256
SLIDE_WINDOW = 4096


eps = 1e-06
softcap = 50.0
negative = -1e30
f32 = jnp.float32
b16 = jnp.bfloat16


def rms_scale(value_rows):
    return lax.rsqrt(jnp.mean(value_rows * value_rows, axis=-1, keepdims=True) + eps)


def rms_back(grad, normed, scale):
    return scale * (grad - normed * jnp.mean(grad * normed, axis=-1, keepdims=True))


def rotary_tables(positions):
    inverse = 1.0 / 10000.0 ** (jnp.arange(0, HEAD_SIZE, 2, dtype=f32) / HEAD_SIZE)
    angles = positions.astype(f32)[:, None] * inverse[None, :]
    return (jnp.cos(angles), jnp.sin(angles))


def apply_rotary(value_rows, cosine_table, sine_table):
    half = value_rows.shape[-1] // 2
    first, second = value_rows[:, :half], value_rows[:, half:]
    return jnp.concatenate(
        [first * cosine_table - second * sine_table, second * cosine_table + first * sine_table],
        axis=-1,
    )


def rotate_back(grads, cosine_table, sine_table):
    return apply_rotary(grads, cosine_table, -sine_table)


def gated(gate_value, up_value):
    return jax.nn.gelu(gate_value, approximate=True) * up_value


def exchange(blocks, axis):
    return lax.all_to_all(blocks, axis, 0, 0, tiled=True)


def gathered(block, axis):
    count = lax.axis_size(axis)
    return exchange(jnp.broadcast_to(block[None], (count,) + block.shape), axis)


def swapped(value, axis, bit):
    count = lax.axis_size(axis)
    return lax.ppermute(value, axis, [(place, place ^ bit) for place in range(count)])


def passed_on(value, steps, way):
    n = lax.axis_size("dp")
    pairs = [(s, s + 1) for s in range(steps - 1, n - 1)]
    if way < 0:
        pairs = [(n - 1 - s, n - 1 - t) for s, t in pairs]
    return lax.ppermute(value, "dp", pairs)


def shifted(value, axis, steps):
    count = lax.axis_size(axis)
    return lax.ppermute(
        value, axis, [(s, s + steps) for s in range(count) if 0 <= s + steps < count]
    )


def summed(blocks):
    return jnp.sum(blocks.astype(f32), axis=0)


def dot(left, right):
    return jnp.dot(left, right, preferred_element_type=f32)


def dot_nt(left, right):
    return lax.dot_general(left, right, (((1,), (1,)), ((), ())), preferred_element_type=f32)


def dot_tn(left, right):
    return lax.dot_general(left, right, (((0,), (0,)), ((), ())), preferred_element_type=f32)


def rotated(value, steps):
    n = lax.axis_size("dp")
    return lax.ppermute(value, "dp", [(s, (s + steps) % n) for s in range(n)])


def picked(first, pair):
    low, high = pair
    return jnp.where(first, low, high), jnp.where(first, high, low)


def after(value, *earlier):
    return lax.optimization_barrier((value,) + earlier)[0]


def ring_blocks(block):
    n = lax.axis_size("dp")
    return [block] + [rotated(block, steps) for steps in range(1, n)]


def in_order(blocks):
    n = lax.axis_size("dp")
    place = lax.axis_index("dp")
    blocks = [blocks[-j % n] for j in range(n)]
    for bit in range((n - 1).bit_length()):
        shift = 1 << bit
        odd = (place >> bit) % 2 == 1
        blocks = [jnp.where(odd, blocks[(j - shift) % n], blocks[j]) for j in range(n)]
    return jnp.stack(blocks)


def ring_summed(blocks, *earlier):
    n = lax.axis_size("dp")
    place = lax.axis_index("dp")
    total = lax.dynamic_index_in_dim(blocks, place, 0, keepdims=False).astype(f32)
    got = [
        rotated(
            lax.dynamic_index_in_dim(blocks, (place + steps) % n, 0, keepdims=False), steps
        )
        for steps in range(1, n)
    ]
    got = after(got, *earlier)
    for block in got:
        total = total + block.astype(f32)
    return total


def unit_blocks(weights, side, n):
    deep, total = weights[0].shape
    units = total // n
    shape = (n, deep // 2, units)
    if deep % 32:
        halves = [lax.dynamic_slice_in_dim(w, side * (deep // 2), deep // 2) for w in weights]
        return [jnp.swapaxes(w.reshape(deep // 2, n, units), 0, 1) for w in halves]

    def kernel(side_ref, *refs):
        for source, target in zip(refs[: len(weights)], refs[len(weights) :]):
            for j in range(n):
                target[j] = source[:, j * units : (j + 1) * units]

    return pl.pallas_call(
        kernel,
        grid_spec=pltpu.PrefetchScalarGridSpec(
            num_scalar_prefetch=1,
            grid=(1,),
            in_specs=[pl.BlockSpec((deep // 2, total), lambda g, s: (s[0], 0))] * len(weights),
            out_specs=[pl.BlockSpec(shape, lambda g, s: (0, 0, 0))] * len(weights),
        ),
        out_shape=[jax.ShapeDtypeStruct(shape, w.dtype) for w in weights],
        compiler_params=pltpu.CompilerParams(vmem_limit_bytes=48 << 20),
        name="unit_blocks",
    )(side.astype(jnp.int32).reshape(1), *weights)


def side_by_side(blocks):
    n, rows, units = blocks.shape
    if rows % 16:
        return jnp.swapaxes(blocks, 0, 1).reshape(rows, n * units).astype(f32)

    def kernel(source, target):
        for j in range(n):
            target[:, j * units : (j + 1) * units] = source[j].astype(f32)

    return pl.pallas_call(
        kernel,
        out_shape=jax.ShapeDtypeStruct((rows, n * units), f32),
        compiler_params=params(16),
        name="side_by_side",
    )(blocks)


def bits():
    lane = lax.axis_index("tensor")
    return lax.axis_index("context") == 0, lane < 2, lane % 2 == 0


AXES = (("context", 1), ("tensor", 2), ("tensor", 1))


def join(own, step, axis):
    low, high = picked(bits()[step], (own, swapped(own, *AXES[step])))
    return jnp.stack([low, high], axis=axis)


def fold(partial, step, axis):
    low = lax.index_in_dim(partial, 0, axis, keepdims=False)
    high = lax.index_in_dim(partial, 1, axis, keepdims=False)
    kept, sent = picked(bits()[step], (low, high))
    return kept + swapped(sent.astype(b16), *AXES[step]).astype(f32)


def half_sent(partial, step, axis):
    low = lax.index_in_dim(partial, 0, axis, keepdims=False)
    high = lax.index_in_dim(partial, 1, axis, keepdims=False)
    kept, sent = picked(bits()[step], (low, high))
    return kept, swapped(sent.astype(b16), *AXES[step])


def collect_group(partial, sub, *earlier):
    width = partial.shape[-1]
    partial = after(fold(partial.reshape(2, 2, 2, sub, width), 2, 2), *earlier)
    left, right = partial[..., : width // 2], partial[..., width // 2 :]
    left = fold(fold(left, 0, 0), 1, 0)
    right = fold(fold(right, 1, 1), 0, 0)
    return jnp.concatenate([left, right], axis=-1)


SMEM = pltpu.SMEM
VMEM = pltpu.VMEM


def params(megabytes=48):
    return pltpu.CompilerParams(vmem_limit_bytes=megabytes << 20)


def scalar(value):
    return value.astype(jnp.int32).reshape(1)


def whole(shape):
    return pl.BlockSpec(shape, lambda *_: (0,) * len(shape))


def fused(function, flags, *args):
    shapes = jax.eval_shape(function, *flags, *args)
    leaves, tree = jax.tree.flatten(shapes)
    size = sum(math.prod(v.shape) * v.dtype.itemsize for v in (*args, *leaves))
    if size > 32 << 20:
        return function(*flags, *args)
    count = len(flags)

    def kernel(*refs):
        given = [ref[0] == 1 for ref in refs[:count]]
        given += [ref[...] for ref in refs[count : count + len(args)]]
        results = jax.tree.leaves(function(*given))
        for ref, result in zip(refs[count + len(args) :], results):
            ref[...] = result

    out = pl.pallas_call(
        kernel,
        in_specs=[pl.BlockSpec(memory_space=SMEM)] * count
        + [pl.BlockSpec(memory_space=VMEM)] * len(args),
        out_specs=[pl.BlockSpec(memory_space=VMEM)] * len(leaves),
        out_shape=leaves,
        compiler_params=params(8 + (size >> 20)),
        name="fused_" + getattr(function, "__name__", "part").strip("<>_"),
    )(*[scalar(flag) for flag in flags], *args)
    return jax.tree.unflatten(tree, out)


def join_kernel(own, step, axis):
    return put_together(own, swapped(own, *AXES[step]), bits()[step], axis)


def put_together(own, other, first, axis):
    if own.ndim < 2 or own.shape[-2] % 16:
        return jnp.stack(picked(first, (own, other)), axis=axis)
    shape = own.shape[:axis] + (2,) + own.shape[axis:]

    def kernel(place, own_ref, other_ref, out):
        lead = (slice(None),) * axis
        out[(*lead, place[0])] = own_ref[...]
        out[(*lead, 1 - place[0])] = other_ref[...]

    return pl.pallas_call(
        kernel,
        in_specs=[pl.BlockSpec(memory_space=SMEM)] + [pl.BlockSpec(memory_space=VMEM)] * 2,
        out_specs=pl.BlockSpec(memory_space=VMEM),
        out_shape=jax.ShapeDtypeStruct(shape, own.dtype),
        compiler_params=params(8),
        name="join",
    )(1 - scalar(first), own, other)


def parted(first, low, high):
    kept, sent = picked(first, (low, high))
    return kept, sent.astype(b16)


def core_parted(low_core, out, sub):
    parts = [out[k * sub : (k + 1) * sub] for k in range(8)]
    pairs = [parted(low_core, parts[2 * k], parts[2 * k + 1]) for k in range(4)]
    return tuple(
        jnp.concatenate([pair[which] for pair in pairs], axis=0).reshape(2, 2, sub, -1)
        for which in range(2)
    )


def collect_halves(kept, sent, *earlier):
    half = kept.shape[-1] // 2
    context, high, low = bits()

    def halve(context, high, kept, got):
        total = kept + got.astype(f32)
        left, right = total[..., :half], total[..., half:]
        left = parted(context, left[0], left[1])
        right = parted(high, right[:, 0], right[:, 1])
        return *left, *right

    def again(context, high, left, left_got, right, right_got):
        left = left + left_got.astype(f32)
        right = right + right_got.astype(f32)
        return *parted(high, left[0], left[1]), *parted(context, right[0], right[1])

    got = swapped(sent, *AXES[2])
    left, left_sent, right, right_sent = fused(halve, (context, high), kept, got)
    left_sent, right_sent = after((left_sent, right_sent), *earlier)
    left_got, right_got = swapped(left_sent, *AXES[0]), swapped(right_sent, *AXES[1])
    left, left_sent, right, right_sent = fused(
        again, (context, high), left, left_got, right, right_got
    )
    return left, swapped(left_sent, *AXES[1]), right, swapped(right_sent, *AXES[0])


def halves_summed(left, left_got, right, right_got):
    return jnp.concatenate([left + left_got.astype(f32), right + right_got.astype(f32)], axis=-1)


def side_by_side_columns(left, right):
    return jnp.concatenate([left, right], axis=-1)


def spread_group(block):
    width = block.shape[-1]
    left, right = block[:, : width // 2], block[:, width // 2 :]
    left = join_kernel(join_kernel(left, 0, 0), 1, 1)
    right = join_kernel(join_kernel(right, 1, 0), 0, 0)
    return join_kernel(fused(side_by_side_columns, (), left, right), 2, 2).reshape(-1, width)


def spread_lanes(block):
    return join_kernel(join_kernel(block, 1, 0), 2, 1).reshape(-1, block.shape[-1])


def row_grad(left, right):
    width = left.shape[1]
    step = 384

    def kernel(left_ref, right_ref, out):
        for start in range(0, width, step):
            here = slice(start, start + step)
            out[here, :] = dot_tn(left_ref[:, here], right_ref[...]).astype(b16)

    return pl.pallas_call(
        kernel,
        out_shape=jax.ShapeDtypeStruct((width, right.shape[1]), b16),
        compiler_params=params(16),
        name="row_grad",
    )(left, right)


def attend_back(rows, w_out, keys, values, queries, probs, bent, tables, side):
    group, width = rows.shape
    span, size = keys.shape
    block = 128
    steps = group // block

    def kernel(
        side_ref, rows_ref, out_ref, key_ref, value_ref, query_ref, probs_ref, bent_ref, cos_ref, sin_ref,
        query_grad, kept, sent, key_sum, value_sum,
    ):
        step = pl.program_id(0)
        mixed = dot(rows_ref[...], out_ref[...]).astype(b16)
        grads = dot_nt(mixed, value_ref[...])
        probs = probs_ref[...]
        bent = bent_ref[...]
        grads = probs * (grads - jnp.sum(probs * grads, axis=-1, keepdims=True))
        grads = (grads * (1.0 - bent * bent)).astype(b16)
        turned = rotate_back(dot(grads, key_ref[...]), cos_ref[...], sin_ref[...])
        query_grad[...] = (turned * HEAD_SIZE ** (-0.5)).astype(b16)
        key_part = dot_tn(grads, query_ref[...])
        value_part = dot_tn(probs.astype(b16), mixed)

        @pl.when(step == 0)
        def _():
            key_sum[...] = key_part
            value_sum[...] = value_part

        @pl.when(step > 0)
        def _():
            key_sum[...] += key_part
            value_sum[...] += value_part

        @pl.when((step == steps - 1) & (side_ref[0] == 0))
        def _():
            kept[...] = key_sum[...]
            sent[...] = value_sum[...].astype(b16)

        @pl.when((step == steps - 1) & (side_ref[0] == 1))
        def _():
            kept[...] = value_sum[...]
            sent[...] = key_sum[...].astype(b16)

    def by_rows(columns):
        return pl.BlockSpec((block, columns), lambda g: (g, 0))

    return pl.pallas_call(
        kernel,
        grid=(steps,),
        in_specs=[
            pl.BlockSpec(memory_space=SMEM),
            by_rows(width),
            whole((width, size)),
            whole((span, size)),
            whole((span, size)),
            by_rows(size),
            by_rows(span),
            by_rows(span),
            by_rows(size // 2),
            by_rows(size // 2),
        ],
        out_specs=[by_rows(size), whole((span, size)), whole((span, size))],
        out_shape=[
            jax.ShapeDtypeStruct((group, size), b16),
            jax.ShapeDtypeStruct((span, size), f32),
            jax.ShapeDtypeStruct((span, size), b16),
        ],
        scratch_shapes=[pltpu.VMEM((span, size), f32)] * 2,
        compiler_params=params(),
        name="attend_back",
    )(scalar(side), rows, w_out, keys, values, queries, probs, bent, *tables)


def together(*values):
    return lax.optimization_barrier(values)


def added(terms):
    total = terms[0].astype(f32)
    for term in terms[1:]:
        total = total + term.astype(f32)
    return total


def spread_chunk(block, *earlier):
    block = jnp.concatenate([block, swapped(block, "tensor", 2)], axis=0)
    block = after(block, *earlier)
    return jnp.concatenate([block, swapped(block, "tensor", 1)], axis=0)


def folded(partial, bit):
    half = partial.shape[0] // 2
    return partial[:half] + swapped(partial[half:].astype(b16), "tensor", bit).astype(f32)


def pipelined(block, work):
    n = lax.axis_size("dp")
    sub = block.shape[0]
    groups = [[0], [1, n - 1], list(range(2, n - 1))] if n > 3 else [[0], list(range(1, n))]
    rows, partial, rest = [], [], []
    sent = block
    for group in groups:
        got = [rotated(sent, steps) if steps else block for steps in group]
        if group[0]:
            sent = after(block, *got)
        rows.append(got)
    near = rows[1]
    for number, got in enumerate(rows):
        got = jnp.concatenate(got, axis=0) if len(got) > 1 else got[0]
        rows[number] = spread_chunk(got, *partial[:1])
        first, *others = work(number, after(rows[number], *partial[-1:]), *near)
        partial.append(first)
        rest.append(others)

    terms, earlier = [], []
    for number in list(range(1, len(groups))) + [0]:
        back = after(folded(partial[number], 1), *earlier)
        back = folded(back, 2)
        earlier = [back]
        for place, steps in enumerate(groups[number]):
            part = back[place * sub : (place + 1) * sub]
            terms.append(rotated(part.astype(b16), -steps) if steps else part)
    return rows, terms, list(zip(*rest)), partial + earlier


def on_device(
    tokens,
    segments,
    w_query,
    key_weight,
    value_weight,
    w_output,
    w_gate,
    w_up,
    w_down,
    pre_attn_gain,
    post_attn_gain,
    pre_ffw_gain,
    post_ffw_gain,
    cotangent,
):
    n = lax.axis_size("dp")
    place = lax.axis_index("dp")
    side = lax.axis_index("context")
    lane = lax.axis_index("tensor")
    lanes = lax.axis_size("tensor")
    rows, width = tokens.shape
    group = 2 * rows
    sub = rows // lanes
    deep = width // n
    reach = min((SLIDE_WINDOW + group - 2) // group, n - 1)
    is_first = side == 0

    def half_of(value, which, axis):
        size = value.shape[axis] // 2
        low = lax.slice_in_dim(value, 0, size, axis=axis)
        high = lax.slice_in_dim(value, size, 2 * size, axis=axis)
        return jnp.where(which == 0, low, high)

    def with_rider(block, values):
        rider = jnp.zeros((16 * HEAD_SIZE - values.size,), b16)
        rider = jnp.concatenate([values.astype(b16).reshape(-1), rider])
        return jnp.concatenate([block, rider.reshape(16, HEAD_SIZE)], axis=0)

    def split_rider(blocks, count):
        size = blocks.shape[1] - 16
        rider = blocks[:, size:].reshape(blocks.shape[0], -1)[:, :count]
        return blocks[:, :size], rider

    gains = jnp.concatenate([pre_attn_gain, post_attn_gain, pre_ffw_gain, post_ffw_gain])
    pair_got = ring_blocks(with_rider(jnp.where(is_first, key_weight, value_weight), gains))
    group_tokens = join(tokens, 0, 0).reshape(group, width)
    segment_pair = join(segments[None].astype(b16), 0, 0)
    pair_in, gains = split_rider(in_order(pair_got), 4 * deep)
    pair_in = pair_in.reshape(width, HEAD_SIZE)
    gains = 1.0 + jnp.swapaxes(gains.reshape(n, 4, deep), 0, 1).reshape(4, width).astype(f32)
    normed_one = group_tokens.astype(f32)
    normed_one = normed_one * rms_scale(normed_one)
    lifted_one = (normed_one * gains[0]).astype(b16)
    positions = place * group + jnp.arange(group, dtype=jnp.int32)
    cosine_table, sine_table = rotary_tables(positions)
    mine = dot(lifted_one, pair_in)
    mine = jnp.where(is_first, apply_rotary(mine, cosine_table, sine_table), mine).astype(b16)
    mine = [mine] + [shifted(mine, "dp", steps) for steps in range(1, reach + 1)]
    query_got = ring_blocks(after(with_rider(half_of(w_query, side, 1), segment_pair), mine[0]))
    query_in, all_segments = split_rider(in_order(query_got), group)
    query_in = query_in.reshape(width, HEAD_SIZE)
    all_segments = all_segments.reshape(-1).astype(jnp.int32)
    out_got = ring_blocks(after(half_of(w_output.T, side, 1), *query_got))
    w_out = in_order(out_got).reshape(width, HEAD_SIZE)

    units = w_gate.shape[1] // n
    gate_got, up_got, down_got = unit_blocks([w_gate, w_up, w_down.T], side, n)
    gate_got = exchange(after(gate_got, *mine), "dp")
    up_got = exchange(after(up_got, gate_got), "dp")
    down_got = exchange(after(down_got, up_got), "dp")
    gate_other, up_other, down_other = [
        swapped(got, "context", 1) for got in (gate_got, up_got, down_got)
    ]

    def both_halves(own, other):
        return put_together(own, other, is_first, 1).reshape(width, units)

    theirs = [swapped(block, "context", 1) for block in mine]
    mine = jnp.concatenate(mine[::-1], axis=0)
    theirs = jnp.concatenate(theirs[::-1], axis=0)
    keys = jnp.where(is_first, mine, theirs)
    values = jnp.where(is_first, theirs, mine)
    queries = (
        apply_rotary(dot(lifted_one, query_in), cosine_table, sine_table) * HEAD_SIZE ** (-0.5)
    ).astype(b16)
    span = (reach + 1) * group
    key_positions = (place - reach) * group + jnp.arange(span, dtype=jnp.int32)
    padded = jnp.concatenate([jnp.full((reach * group,), -1, jnp.int32), all_segments])
    key_segments = lax.dynamic_slice_in_dim(padded, place * group, span)
    query_segments = key_segments[reach * group :]
    valid = (key_positions[None, :] <= positions[:, None]) & (
        positions[:, None] - key_positions[None, :] < SLIDE_WINDOW
    )
    valid = valid & (key_positions[None, :] >= 0)
    valid = valid & (key_segments[None, :] == query_segments[:, None])
    bent = jnp.tanh(dot_nt(queries, keys) / softcap)
    masked = jnp.where(valid, softcap * bent, negative)
    weights = jnp.exp(masked - jnp.max(masked, axis=-1, keepdims=True))
    probs = weights / jnp.sum(weights, axis=-1, keepdims=True)
    probs_low = probs.astype(b16)
    mixed = dot(after(probs_low, gate_got, *out_got), values).astype(b16)
    low_core = bits()[2]

    def out_product(low_core, mixed, w_out):
        return core_parted(low_core, dot_nt(mixed, w_out), sub)

    branch = collect_halves(*fused(out_product, (low_core,), mixed, w_out), gate_other)
    branch = after(halves_summed(*branch), up_got, gate_other)

    own_tokens = lax.dynamic_slice_in_dim(tokens, lane * sub, sub)
    own_cotangent = lax.dynamic_slice_in_dim(cotangent, lane * sub, sub)
    grad_out = own_cotangent.astype(f32)
    scale_two = rms_scale(branch)
    normed_two = branch * scale_two
    middle = own_tokens.astype(f32) + normed_two * gains[1]
    scale_three = rms_scale(middle)
    normed_three = middle * scale_three
    lifted_two = after((normed_three * gains[2]).astype(b16), down_got, up_other)
    gate_w = both_halves(gate_got, gate_other)
    up_w = both_halves(up_got, up_other)

    def feed(number, chunk, *arrived):
        down_w = both_halves(down_got, after(down_other, *arrived))
        gate = dot(chunk, gate_w)
        upper = dot(chunk, up_w)
        hidden = gated(gate, upper).astype(b16)
        return dot_nt(hidden, down_w), gate, upper, hidden

    lifted_two, terms, (gate, upper, hidden), unused = pipelined(lifted_two, feed)
    down = added(terms)
    scale_four = rms_scale(down)
    normed_four = down * scale_four
    output = (middle + normed_four * gains[3]).astype(b16)

    grad_gain_four = jnp.sum(grad_out * normed_four, axis=0, keepdims=True)
    def unit_grad(left, right):
        partial = dot_tn(jnp.concatenate(left, axis=0), jnp.concatenate(right, axis=0))
        return partial.reshape(n, 2, deep // 2, units)

    grad_down = rms_back(grad_out * gains[3], normed_four, scale_four).astype(b16)
    down_w = both_halves(down_got, down_other)

    def feed_back(number, chunk, *arrived):
        unused, pull = jax.vjp(gated, gate[number], upper[number])
        grad_gate, grad_upper = [side.astype(b16) for side in pull(dot(chunk, down_w))]
        partial = dot_nt(grad_gate, gate_w) + dot_nt(grad_upper, up_w)
        return partial, grad_gate, grad_upper

    grad_down, terms, (grad_gate, grad_upper), partial = pipelined(grad_down, feed_back)
    output = spread_lanes(after(output, grad_down[0]))
    down_sum = unit_grad(grad_down, after(hidden, partial[-3]))
    down_kept, down_got = half_sent(down_sum, 0, 1)

    def both_parts(total):
        kept, sent = picked(is_first, (total[:, 0], total[:, 1]))
        return kept, sent.astype(b16)

    gate_sum = unit_grad(lifted_two, after(grad_gate, partial[-1]))
    up_sum = unit_grad(lifted_two, after(grad_upper, partial[-1]))
    gate_kept, gate_sent = both_parts(gate_sum)
    up_kept, up_sent = both_parts(up_sum)
    terms, down_got, gate_sent = together(terms, down_got, gate_sent)

    def two_sided(kept, got):
        return (kept + got.astype(f32)).astype(b16)

    def middle_back(cotangent, gains, scale_two, normed_two, scale_three, normed_three, *terms):
        grad_out = cotangent.astype(f32)
        lifted_grad = added(terms)
        grad_middle = grad_out + rms_back(lifted_grad * gains[2:3], normed_three, scale_three)
        grad_branch = rms_back(grad_middle * gains[1:2], normed_two, scale_two).astype(b16)
        gain_two = jnp.sum(grad_middle * normed_two, axis=0, keepdims=True)
        gain_three = jnp.sum(lifted_grad * normed_three, axis=0, keepdims=True)
        return grad_middle, grad_branch, gain_two, gain_three

    down_part = (down_kept + down_got.astype(f32)).astype(b16)
    grad_w_down = exchange(down_part, "dp")
    gate_got = swapped(gate_sent, "context", 1)
    grad_middle, grad_branch, grad_gain_two, grad_gain_three = fused(
        middle_back, (), own_cotangent, gains, scale_two, normed_two, scale_three, normed_three, *terms
    )
    grad_branch, grad_w_down, gate_got = together(grad_branch, grad_w_down, gate_got)
    gate_part = (gate_kept + gate_got.astype(f32)).astype(b16)


    def row_blocks(left, right):
        return row_grad(left, right).reshape(n, deep, HEAD_SIZE)

    grad_w_gate = exchange(gate_part, "dp")
    up_got = swapped(after(up_sent, gate_got), "context", 1)
    grad_branch = spread_group(grad_branch)
    out_blocks = row_blocks(grad_branch, mixed)
    grad_query_pre, kept, sent = attend_back(
        grad_branch, w_out, keys, values, queries, probs, bent, (cosine_table, sine_table), side
    )
    query_blocks = row_blocks(lifted_one, grad_query_pre)
    up_got, kept = together(up_got, kept)
    up_part = (up_kept + up_got.astype(f32)).astype(b16)
    grad_w_up = exchange(after(up_part, grad_w_gate), "dp")
    out_blocks, query_blocks, output = together(
        after(out_blocks, grad_w_gate), query_blocks, output
    )
    kept = kept.reshape(reach + 1, group, HEAD_SIZE)
    sent = sent.reshape(reach + 1, group, HEAD_SIZE)

    def full(kept, got):
        return kept + got.astype(f32)

    slots = [
        fused(two_sided if slot < reach else full, (), kept[slot], swapped(sent[slot], "context", 1))
        for slot in range(reach + 1)
    ]
    grad_w_out = ring_summed(out_blocks)
    terms = [slots[reach]]
    for steps in range(reach, 0, -1):
        terms.append(shifted(slots[reach - steps], "dp", -steps))
    terms, grad_w_up, grad_w_out = together(terms, grad_w_up, grad_w_out)

    def unturned(is_first, cosine, sine, *terms):
        total = added(terms)
        return jnp.where(is_first, rotate_back(total, cosine, sine), total).astype(b16)

    mine = fused(unturned, (is_first,), cosine_table, sine_table, *terms)
    pair_blocks = row_blocks(lifted_one, mine)

    def first_product(low_core, tokens, query_grad, query_in, pair_grad, pair_in):
        out = dot_nt(query_grad, query_in) + dot_nt(pair_grad, pair_in)
        values = tokens.astype(f32)
        gain = jnp.sum(out * (values * rms_scale(values)), axis=0, keepdims=True)
        return *core_parted(low_core, out, sub), gain

    kept, sent, grad_gain_one = fused(
        first_product,
        (low_core,),
        group_tokens,
        grad_query_pre,
        query_in,
        after(mine, pair_blocks),
        pair_in,
    )
    first_grad = collect_halves(kept, sent)

    def first_back(own_tokens, gains, grad_middle, *halves):
        first_grad = halves_summed(*halves)
        values = own_tokens.astype(f32)
        scale = rms_scale(values)
        return (grad_middle + rms_back(first_grad * gains[:1], values * scale, scale)).astype(b16)

    grad_inputs = fused(first_back, (), own_tokens, gains, grad_middle, *first_grad)
    grad_gains = jnp.concatenate(
        [grad_gain_one, grad_gain_two, grad_gain_three, grad_gain_four], axis=0
    )

    def halves(total):
        kept, sent = picked(is_first, (total[: deep // 2], total[deep // 2 : deep]))
        return kept, swapped(sent.astype(b16), "context", 1).astype(f32)

    grad_w_query = ring_summed(after(query_blocks, *terms), grad_inputs)
    grad_pair = ring_summed(pair_blocks, grad_inputs)
    grad_gains = after(grad_gains, grad_inputs)
    grad_gains = grad_gains + swapped(grad_gains, "tensor", 2)
    grad_gains = grad_gains + swapped(grad_gains, "tensor", 1)
    grad_gains = jnp.transpose(grad_gains.reshape(4, n, 2, deep // 2), (2, 1, 0, 3))
    grad_gains, sent = picked(is_first, (grad_gains[0], grad_gains[1]))
    grad_gains = ring_summed(grad_gains + swapped(sent, "context", 1))
    grad_inputs = spread_lanes(grad_inputs).astype(f32)
    grad_w_out = jnp.concatenate(picked(is_first, halves(grad_w_out)), axis=1).T
    grad_w_query = jnp.concatenate(picked(is_first, halves(grad_w_query)), axis=1)
    grad_w_key, grad_w_value = picked(is_first, halves(grad_pair))
    grad_w_down, grad_w_gate, grad_w_up = after(
        (grad_w_down, grad_w_gate, grad_w_up), mine
    )
    grad_w_down = side_by_side(grad_w_down).T
    grad_w_gate = side_by_side(grad_w_gate)
    grad_w_up = side_by_side(grad_w_up)
    return (
        output,
        grad_inputs,
        grad_w_query,
        grad_w_key,
        grad_w_value,
        grad_w_out,
        grad_w_gate,
        grad_w_up,
        grad_w_down,
        grad_gains[0],
        grad_gains[1],
        grad_gains[2],
        grad_gains[3],
    )


def solution(mesh):
    return jax.shard_map(
        on_device,
        mesh=mesh,
        in_specs=(
            P(("dp", "context"), None),
            P(("dp", "context")),
            P("dp", "tensor"),
            P("dp", "tensor"),
            P("dp", "tensor"),
            P("tensor", "dp"),
            P("dp", "tensor"),
            P("dp", "tensor"),
            P("tensor", "dp"),
            P("dp"),
            P("dp"),
            P("dp"),
            P("dp"),
            P(("dp", "context"), None),
        ),
        out_specs=(
            P(("dp", "context"), None),
            P(("dp", "context"), None),
            P(("dp", "context"), "tensor"),
            P(("dp", "context"), "tensor"),
            P(("dp", "context"), "tensor"),
            P("tensor", ("dp", "context")),
            P(("dp", "context"), "tensor"),
            P(("dp", "context"), "tensor"),
            P("tensor", ("dp", "context")),
            P(("dp", "context")),
            P(("dp", "context")),
            P(("dp", "context")),
            P(("dp", "context")),
        ),
        check_vma=False,
    )
```

```python
import math

import jax
import jax.numpy as jnp
from jax import lax
from jax.experimental import pallas as pl
from jax.experimental.pallas import tpu as pltpu
from jax.sharding import PartitionSpec as P

HEAD_SIZE = 256
SLIDE_WINDOW = 4096


eps = 1e-06
softcap = 50.0
negative = -1e30
f32 = jnp.float32
b16 = jnp.bfloat16


def rms_scale(value_rows):
    return lax.rsqrt(jnp.mean(value_rows * value_rows, axis=-1, keepdims=True) + eps)


def rms_back(grad, normed, scale):
    return scale * (grad - normed * jnp.mean(grad * normed, axis=-1, keepdims=True))


def rotary_tables(positions):
    inverse = 1.0 / 10000.0 ** (jnp.arange(0, HEAD_SIZE, 2, dtype=f32) / HEAD_SIZE)
    angles = positions.astype(f32)[:, None] * inverse[None, :]
    return (jnp.cos(angles), jnp.sin(angles))


def apply_rotary(value_rows, cosine_table, sine_table):
    half = value_rows.shape[-1] // 2
    first, second = value_rows[:, :half], value_rows[:, half:]
    return jnp.concatenate(
        [first * cosine_table - second * sine_table, second * cosine_table + first * sine_table],
        axis=-1,
    )


def rotate_back(grads, cosine_table, sine_table):
    return apply_rotary(grads, cosine_table, -sine_table)


def gated(gate_value, up_value):
    return jax.nn.gelu(gate_value, approximate=True) * up_value


def exchange(blocks, axis):
    return lax.all_to_all(blocks, axis, 0, 0, tiled=True)


def gathered(block, axis):
    count = lax.axis_size(axis)
    return exchange(jnp.broadcast_to(block[None], (count,) + block.shape), axis)


def swapped(value, axis, bit):
    count = lax.axis_size(axis)
    return lax.ppermute(value, axis, [(place, place ^ bit) for place in range(count)])


def passed_on(value, steps, way):
    n = lax.axis_size("dp")
    pairs = [(s, s + 1) for s in range(steps - 1, n - 1)]
    if way < 0:
        pairs = [(n - 1 - s, n - 1 - t) for s, t in pairs]
    return lax.ppermute(value, "dp", pairs)


def shifted(value, axis, steps):
    count = lax.axis_size(axis)
    return lax.ppermute(
        value, axis, [(s, s + steps) for s in range(count) if 0 <= s + steps < count]
    )


def summed(blocks):
    return jnp.sum(blocks.astype(f32), axis=0)


def dot(left, right):
    return jnp.dot(left, right, preferred_element_type=f32)


def dot_nt(left, right):
    return lax.dot_general(left, right, (((1,), (1,)), ((), ())), preferred_element_type=f32)


def dot_tn(left, right):
    return lax.dot_general(left, right, (((0,), (0,)), ((), ())), preferred_element_type=f32)


def rotated(value, steps):
    n = lax.axis_size("dp")
    return lax.ppermute(value, "dp", [(s, (s + steps) % n) for s in range(n)])


def picked(first, pair):
    low, high = pair
    return jnp.where(first, low, high), jnp.where(first, high, low)


def after(value, *earlier):
    return lax.optimization_barrier((value,) + earlier)[0]


def ring_blocks(block):
    n = lax.axis_size("dp")
    return [block] + [rotated(block, steps) for steps in range(1, n)]


def in_order(blocks):
    n = lax.axis_size("dp")
    place = lax.axis_index("dp")
    blocks = [blocks[-j % n] for j in range(n)]
    for bit in range((n - 1).bit_length()):
        shift = 1 << bit
        odd = (place >> bit) % 2 == 1
        blocks = [jnp.where(odd, blocks[(j - shift) % n], blocks[j]) for j in range(n)]
    return jnp.stack(blocks)


def ring_summed(blocks, *earlier):
    n = lax.axis_size("dp")
    place = lax.axis_index("dp")
    total = lax.dynamic_index_in_dim(blocks, place, 0, keepdims=False).astype(f32)
    got = [
        rotated(
            lax.dynamic_index_in_dim(blocks, (place + steps) % n, 0, keepdims=False), steps
        )
        for steps in range(1, n)
    ]
    got = after(got, *earlier)
    for block in got:
        total = total + block.astype(f32)
    return total


def unit_blocks(weights, side, n):
    deep, total = weights[0].shape
    units = total // n
    shape = (n, deep // 2, units)
    if deep % 32:
        halves = [lax.dynamic_slice_in_dim(w, side * (deep // 2), deep // 2) for w in weights]
        return [jnp.swapaxes(w.reshape(deep // 2, n, units), 0, 1) for w in halves]

    def kernel(side_ref, *refs):
        for source, target in zip(refs[: len(weights)], refs[len(weights) :]):
            for j in range(n):
                target[j] = source[:, j * units : (j + 1) * units]

    return pl.pallas_call(
        kernel,
        grid_spec=pltpu.PrefetchScalarGridSpec(
            num_scalar_prefetch=1,
            grid=(1,),
            in_specs=[pl.BlockSpec((deep // 2, total), lambda g, s: (s[0], 0))] * len(weights),
            out_specs=[pl.BlockSpec(shape, lambda g, s: (0, 0, 0))] * len(weights),
        ),
        out_shape=[jax.ShapeDtypeStruct(shape, w.dtype) for w in weights],
        compiler_params=pltpu.CompilerParams(vmem_limit_bytes=48 << 20),
        name="unit_blocks",
    )(side.astype(jnp.int32).reshape(1), *weights)


def side_by_side(blocks):
    n, rows, units = blocks.shape
    if rows % 16:
        return jnp.swapaxes(blocks, 0, 1).reshape(rows, n * units).astype(f32)

    def kernel(source, target):
        for j in range(n):
            target[:, j * units : (j + 1) * units] = source[j].astype(f32)

    return pl.pallas_call(
        kernel,
        out_shape=jax.ShapeDtypeStruct((rows, n * units), f32),
        compiler_params=params(16),
        name="side_by_side",
    )(blocks)


def bits():
    lane = lax.axis_index("tensor")
    return lax.axis_index("context") == 0, lane < 2, lane % 2 == 0


AXES = (("context", 1), ("tensor", 2), ("tensor", 1))


def join(own, step, axis):
    low, high = picked(bits()[step], (own, swapped(own, *AXES[step])))
    return jnp.stack([low, high], axis=axis)


def fold(partial, step, axis):
    low = lax.index_in_dim(partial, 0, axis, keepdims=False)
    high = lax.index_in_dim(partial, 1, axis, keepdims=False)
    kept, sent = picked(bits()[step], (low, high))
    return kept + swapped(sent.astype(b16), *AXES[step]).astype(f32)


def half_sent(partial, step, axis):
    low = lax.index_in_dim(partial, 0, axis, keepdims=False)
    high = lax.index_in_dim(partial, 1, axis, keepdims=False)
    kept, sent = picked(bits()[step], (low, high))
    return kept, swapped(sent.astype(b16), *AXES[step])


def collect_group(partial, sub, *earlier):
    width = partial.shape[-1]
    partial = after(fold(partial.reshape(2, 2, 2, sub, width), 2, 2), *earlier)
    left, right = partial[..., : width // 2], partial[..., width // 2 :]
    left = fold(fold(left, 0, 0), 1, 0)
    right = fold(fold(right, 1, 1), 0, 0)
    return jnp.concatenate([left, right], axis=-1)


SMEM = pltpu.SMEM
VMEM = pltpu.VMEM


def params(megabytes=48):
    return pltpu.CompilerParams(vmem_limit_bytes=megabytes << 20)


def scalar(value):
    return value.astype(jnp.int32).reshape(1)


def whole(shape):
    return pl.BlockSpec(shape, lambda *_: (0,) * len(shape))


def fused(function, flags, *args):
    shapes = jax.eval_shape(function, *flags, *args)
    leaves, tree = jax.tree.flatten(shapes)
    size = sum(math.prod(v.shape) * v.dtype.itemsize for v in (*args, *leaves))
    if size > 32 << 20:
        return function(*flags, *args)
    count = len(flags)

    def kernel(*refs):
        given = [ref[0] == 1 for ref in refs[:count]]
        given += [ref[...] for ref in refs[count : count + len(args)]]
        results = jax.tree.leaves(function(*given))
        for ref, result in zip(refs[count + len(args) :], results):
            ref[...] = result

    out = pl.pallas_call(
        kernel,
        in_specs=[pl.BlockSpec(memory_space=SMEM)] * count
        + [pl.BlockSpec(memory_space=VMEM)] * len(args),
        out_specs=[pl.BlockSpec(memory_space=VMEM)] * len(leaves),
        out_shape=leaves,
        compiler_params=params(8 + (size >> 20)),
        name="fused_" + getattr(function, "__name__", "part").strip("<>_"),
    )(*[scalar(flag) for flag in flags], *args)
    return jax.tree.unflatten(tree, out)


def join_kernel(own, step, axis):
    return put_together(own, swapped(own, *AXES[step]), bits()[step], axis)


def put_together(own, other, first, axis):
    if own.ndim < 2 or own.shape[-2] % 16:
        return jnp.stack(picked(first, (own, other)), axis=axis)
    shape = own.shape[:axis] + (2,) + own.shape[axis:]

    def kernel(place, own_ref, other_ref, out):
        lead = (slice(None),) * axis
        out[(*lead, place[0])] = own_ref[...]
        out[(*lead, 1 - place[0])] = other_ref[...]

    return pl.pallas_call(
        kernel,
        in_specs=[pl.BlockSpec(memory_space=SMEM)] + [pl.BlockSpec(memory_space=VMEM)] * 2,
        out_specs=pl.BlockSpec(memory_space=VMEM),
        out_shape=jax.ShapeDtypeStruct(shape, own.dtype),
        compiler_params=params(8),
        name="join",
    )(1 - scalar(first), own, other)


def parted(first, low, high):
    kept, sent = picked(first, (low, high))
    return kept, sent.astype(b16)


def core_parted(low_core, out, sub):
    parts = [out[k * sub : (k + 1) * sub] for k in range(8)]
    pairs = [parted(low_core, parts[2 * k], parts[2 * k + 1]) for k in range(4)]
    return tuple(
        jnp.concatenate([pair[which] for pair in pairs], axis=0).reshape(2, 2, sub, -1)
        for which in range(2)
    )


def collect_halves(kept, sent, *earlier):
    half = kept.shape[-1] // 2
    context, high, low = bits()

    def halve(context, high, kept, got):
        total = kept + got.astype(f32)
        left, right = total[..., :half], total[..., half:]
        left = parted(context, left[0], left[1])
        right = parted(high, right[:, 0], right[:, 1])
        return *left, *right

    def again(context, high, left, left_got, right, right_got):
        left = left + left_got.astype(f32)
        right = right + right_got.astype(f32)
        return *parted(high, left[0], left[1]), *parted(context, right[0], right[1])

    got = swapped(sent, *AXES[2])
    left, left_sent, right, right_sent = fused(halve, (context, high), kept, got)
    left_sent, right_sent = after((left_sent, right_sent), *earlier)
    left_got, right_got = swapped(left_sent, *AXES[0]), swapped(right_sent, *AXES[1])
    left, left_sent, right, right_sent = fused(
        again, (context, high), left, left_got, right, right_got
    )
    return left, swapped(left_sent, *AXES[1]), right, swapped(right_sent, *AXES[0])


def halves_summed(left, left_got, right, right_got):
    return jnp.concatenate([left + left_got.astype(f32), right + right_got.astype(f32)], axis=-1)


def side_by_side_columns(left, right):
    return jnp.concatenate([left, right], axis=-1)


def spread_group(block):
    width = block.shape[-1]
    left, right = block[:, : width // 2], block[:, width // 2 :]
    left = join_kernel(join_kernel(left, 0, 0), 1, 1)
    right = join_kernel(join_kernel(right, 1, 0), 0, 0)
    return join_kernel(fused(side_by_side_columns, (), left, right), 2, 2).reshape(-1, width)


def spread_lanes(block):
    return join_kernel(join_kernel(block, 1, 0), 2, 1).reshape(-1, block.shape[-1])


def row_grad(left, right):
    width = left.shape[1]
    step = 384

    def kernel(left_ref, right_ref, out):
        for start in range(0, width, step):
            here = slice(start, start + step)
            out[here, :] = dot_tn(left_ref[:, here], right_ref[...]).astype(b16)

    return pl.pallas_call(
        kernel,
        out_shape=jax.ShapeDtypeStruct((width, right.shape[1]), b16),
        compiler_params=params(16),
        name="row_grad",
    )(left, right)


def attend_back(rows, w_out, keys, values, queries, probs, bent, tables, side):
    group, width = rows.shape
    span, size = keys.shape
    block = 128
    steps = group // block

    def kernel(
        side_ref, rows_ref, out_ref, key_ref, value_ref, query_ref, probs_ref, bent_ref, cos_ref, sin_ref,
        query_grad, kept, sent, key_sum, value_sum,
    ):
        step = pl.program_id(0)
        mixed = dot(rows_ref[...], out_ref[...]).astype(b16)
        grads = dot_nt(mixed, value_ref[...])
        probs = probs_ref[...]
        bent = bent_ref[...]
        grads = probs * (grads - jnp.sum(probs * grads, axis=-1, keepdims=True))
        grads = (grads * (1.0 - bent * bent)).astype(b16)
        turned = rotate_back(dot(grads, key_ref[...]), cos_ref[...], sin_ref[...])
        query_grad[...] = (turned * HEAD_SIZE ** (-0.5)).astype(b16)
        key_part = dot_tn(grads, query_ref[...])
        value_part = dot_tn(probs.astype(b16), mixed)

        @pl.when(step == 0)
        def _():
            key_sum[...] = key_part
            value_sum[...] = value_part

        @pl.when(step > 0)
        def _():
            key_sum[...] += key_part
            value_sum[...] += value_part

        @pl.when((step == steps - 1) & (side_ref[0] == 0))
        def _():
            kept[...] = key_sum[...]
            sent[...] = value_sum[...].astype(b16)

        @pl.when((step == steps - 1) & (side_ref[0] == 1))
        def _():
            kept[...] = value_sum[...]
            sent[...] = key_sum[...].astype(b16)

    def by_rows(columns):
        return pl.BlockSpec((block, columns), lambda g: (g, 0))

    return pl.pallas_call(
        kernel,
        grid=(steps,),
        in_specs=[
            pl.BlockSpec(memory_space=SMEM),
            by_rows(width),
            whole((width, size)),
            whole((span, size)),
            whole((span, size)),
            by_rows(size),
            by_rows(span),
            by_rows(span),
            by_rows(size // 2),
            by_rows(size // 2),
        ],
        out_specs=[by_rows(size), whole((span, size)), whole((span, size))],
        out_shape=[
            jax.ShapeDtypeStruct((group, size), b16),
            jax.ShapeDtypeStruct((span, size), f32),
            jax.ShapeDtypeStruct((span, size), b16),
        ],
        scratch_shapes=[pltpu.VMEM((span, size), f32)] * 2,
        compiler_params=params(),
        name="attend_back",
    )(scalar(side), rows, w_out, keys, values, queries, probs, bent, *tables)


def together(*values):
    return lax.optimization_barrier(values)


def added(terms):
    total = terms[0].astype(f32)
    for term in terms[1:]:
        total = total + term.astype(f32)
    return total


def spread_chunk(block, *earlier):
    block = jnp.concatenate([block, swapped(block, "tensor", 2)], axis=0)
    block = after(block, *earlier)
    return jnp.concatenate([block, swapped(block, "tensor", 1)], axis=0)


def folded(partial, bit):
    half = partial.shape[0] // 2
    return partial[:half] + swapped(partial[half:].astype(b16), "tensor", bit).astype(f32)


def pipelined(block, work):
    n = lax.axis_size("dp")
    sub = block.shape[0]
    groups = [[0], [1, n - 1], list(range(2, n - 1))] if n > 3 else [[0], list(range(1, n))]
    rows, partial, rest = [], [], []
    sent = block
    for group in groups:
        got = [rotated(sent, steps) if steps else block for steps in group]
        if group[0]:
            sent = after(block, *got)
        rows.append(got)
    near = rows[1]
    for number, got in enumerate(rows):
        got = jnp.concatenate(got, axis=0) if len(got) > 1 else got[0]
        rows[number] = spread_chunk(got, *partial[:1])
        first, *others = work(number, after(rows[number], *partial[-1:]), *near)
        partial.append(first)
        rest.append(others)

    terms, earlier = [], []
    for number in list(range(1, len(groups))) + [0]:
        back = after(folded(partial[number], 1), *earlier)
        back = folded(back, 2)
        earlier = [back]
        for place, steps in enumerate(groups[number]):
            part = back[place * sub : (place + 1) * sub]
            terms.append(rotated(part.astype(b16), -steps) if steps else part)
    return rows, terms, list(zip(*rest)), partial + earlier


def on_device(
    tokens,
    segments,
    w_query,
    key_weight,
    value_weight,
    w_output,
    w_gate,
    w_up,
    w_down,
    pre_attn_gain,
    post_attn_gain,
    pre_ffw_gain,
    post_ffw_gain,
    cotangent,
):
    n = lax.axis_size("dp")
    place = lax.axis_index("dp")
    side = lax.axis_index("context")
    lane = lax.axis_index("tensor")
    lanes = lax.axis_size("tensor")
    rows, width = tokens.shape
    group = 2 * rows
    sub = rows // lanes
    deep = width // n
    reach = min((SLIDE_WINDOW + group - 2) // group, n - 1)
    is_first = side == 0

    def half_of(value, which, axis):
        size = value.shape[axis] // 2
        low = lax.slice_in_dim(value, 0, size, axis=axis)
        high = lax.slice_in_dim(value, size, 2 * size, axis=axis)
        return jnp.where(which == 0, low, high)

    def with_rider(block, values):
        rider = jnp.zeros((16 * HEAD_SIZE - values.size,), b16)
        rider = jnp.concatenate([values.astype(b16).reshape(-1), rider])
        return jnp.concatenate([block, rider.reshape(16, HEAD_SIZE)], axis=0)

    def split_rider(blocks, count):
        size = blocks.shape[1] - 16
        rider = blocks[:, size:].reshape(blocks.shape[0], -1)[:, :count]
        return blocks[:, :size], rider

    gains = jnp.concatenate([pre_attn_gain, post_attn_gain, pre_ffw_gain, post_ffw_gain])
    pair_got = ring_blocks(jnp.where(is_first, key_weight, value_weight))
    group_tokens = join(tokens, 0, 0).reshape(group, width)
    segment_pair = join(segments[None].astype(b16), 0, 0)
    gains = in_order(ring_blocks(after(gains, segment_pair)))
    pair_in = in_order(pair_got)
    pair_in = pair_in.reshape(width, HEAD_SIZE)
    gains = 1.0 + jnp.swapaxes(gains.reshape(n, 4, deep), 0, 1).reshape(4, width).astype(f32)
    normed_one = group_tokens.astype(f32)
    normed_one = normed_one * rms_scale(normed_one)
    lifted_one = (normed_one * gains[0]).astype(b16)
    positions = place * group + jnp.arange(group, dtype=jnp.int32)
    cosine_table, sine_table = rotary_tables(positions)
    mine = dot(lifted_one, pair_in)
    mine = jnp.where(is_first, apply_rotary(mine, cosine_table, sine_table), mine).astype(b16)
    mine = [mine] + [shifted(mine, "dp", steps) for steps in range(1, reach + 1)]
    query_got = ring_blocks(after(with_rider(half_of(w_query, side, 1), segment_pair), mine[0]))
    query_in, all_segments = split_rider(in_order(query_got), group)
    query_in = query_in.reshape(width, HEAD_SIZE)
    all_segments = all_segments.reshape(-1).astype(jnp.int32)
    out_got = ring_blocks(after(half_of(w_output.T, side, 1), *query_got))
    w_out = in_order(out_got).reshape(width, HEAD_SIZE)

    units = w_gate.shape[1] // n
    gate_got, up_got, down_got = unit_blocks([w_gate, w_up, w_down.T], side, n)
    gate_got = exchange(after(gate_got, *mine), "dp")
    up_got = exchange(after(up_got, gate_got), "dp")
    down_got = exchange(after(down_got, up_got), "dp")
    gate_other, up_other, down_other = [
        swapped(got, "context", 1) for got in (gate_got, up_got, down_got)
    ]

    def both_halves(own, other):
        return put_together(own, other, is_first, 1).reshape(width, units)

    theirs = [swapped(block, "context", 1) for block in mine]
    mine = jnp.concatenate(mine[::-1], axis=0)
    theirs = jnp.concatenate(theirs[::-1], axis=0)
    keys = jnp.where(is_first, mine, theirs)
    values = jnp.where(is_first, theirs, mine)
    queries = (
        apply_rotary(dot(lifted_one, query_in), cosine_table, sine_table) * HEAD_SIZE ** (-0.5)
    ).astype(b16)
    span = (reach + 1) * group
    key_positions = (place - reach) * group + jnp.arange(span, dtype=jnp.int32)
    padded = jnp.concatenate([jnp.full((reach * group,), -1, jnp.int32), all_segments])
    key_segments = lax.dynamic_slice_in_dim(padded, place * group, span)
    query_segments = key_segments[reach * group :]
    valid = (key_positions[None, :] <= positions[:, None]) & (
        positions[:, None] - key_positions[None, :] < SLIDE_WINDOW
    )
    valid = valid & (key_positions[None, :] >= 0)
    valid = valid & (key_segments[None, :] == query_segments[:, None])
    bent = jnp.tanh(dot_nt(queries, keys) / softcap)
    masked = jnp.where(valid, softcap * bent, negative)
    weights = jnp.exp(masked - jnp.max(masked, axis=-1, keepdims=True))
    probs = weights / jnp.sum(weights, axis=-1, keepdims=True)
    probs_low = probs.astype(b16)
    mixed = dot(after(probs_low, gate_got, *out_got), values).astype(b16)
    low_core = bits()[2]

    def out_product(low_core, mixed, w_out):
        return core_parted(low_core, dot_nt(mixed, w_out), sub)

    branch = collect_halves(*fused(out_product, (low_core,), mixed, w_out), gate_other)
    branch = after(halves_summed(*branch), up_got, gate_other)

    own_tokens = lax.dynamic_slice_in_dim(tokens, lane * sub, sub)
    own_cotangent = lax.dynamic_slice_in_dim(cotangent, lane * sub, sub)
    grad_out = own_cotangent.astype(f32)
    scale_two = rms_scale(branch)
    normed_two = branch * scale_two
    middle = own_tokens.astype(f32) + normed_two * gains[1]
    scale_three = rms_scale(middle)
    normed_three = middle * scale_three
    lifted_two = after((normed_three * gains[2]).astype(b16), down_got, up_other)
    gate_w = both_halves(gate_got, gate_other)
    up_w = both_halves(up_got, up_other)

    def feed(number, chunk, *arrived):
        down_w = both_halves(down_got, after(down_other, *arrived))
        gate = dot(chunk, gate_w)
        upper = dot(chunk, up_w)
        hidden = gated(gate, upper).astype(b16)
        return dot_nt(hidden, down_w), gate, upper, hidden

    lifted_two, terms, (gate, upper, hidden), unused = pipelined(lifted_two, feed)
    down = added(terms)
    scale_four = rms_scale(down)
    normed_four = down * scale_four
    output = (middle + normed_four * gains[3]).astype(b16)

    grad_gain_four = jnp.sum(grad_out * normed_four, axis=0, keepdims=True)
    def unit_grad(left, right):
        partial = dot_tn(jnp.concatenate(left, axis=0), jnp.concatenate(right, axis=0))
        return partial.reshape(n, 2, deep // 2, units)

    grad_down = rms_back(grad_out * gains[3], normed_four, scale_four).astype(b16)
    down_w = both_halves(down_got, down_other)

    def feed_back(number, chunk, *arrived):
        unused, pull = jax.vjp(gated, gate[number], upper[number])
        grad_gate, grad_upper = [side.astype(b16) for side in pull(dot(chunk, down_w))]
        partial = dot_nt(grad_gate, gate_w) + dot_nt(grad_upper, up_w)
        return partial, grad_gate, grad_upper

    grad_down, terms, (grad_gate, grad_upper), partial = pipelined(grad_down, feed_back)
    output = spread_lanes(after(output, grad_down[0]))
    down_sum = unit_grad(grad_down, after(hidden, partial[-3]))
    down_kept, down_got = half_sent(down_sum, 0, 1)

    def both_parts(total):
        kept, sent = picked(is_first, (total[:, 0], total[:, 1]))
        return kept, sent.astype(b16)

    gate_sum = unit_grad(lifted_two, after(grad_gate, partial[-1]))
    up_sum = unit_grad(lifted_two, after(grad_upper, partial[-1]))
    gate_kept, gate_sent = both_parts(gate_sum)
    up_kept, up_sent = both_parts(up_sum)
    terms, down_got, gate_sent = together(terms, down_got, gate_sent)

    def two_sided(kept, got):
        return (kept + got.astype(f32)).astype(b16)

    def middle_back(cotangent, gains, scale_two, normed_two, scale_three, normed_three, *terms):
        grad_out = cotangent.astype(f32)
        lifted_grad = added(terms)
        grad_middle = grad_out + rms_back(lifted_grad * gains[2:3], normed_three, scale_three)
        grad_branch = rms_back(grad_middle * gains[1:2], normed_two, scale_two).astype(b16)
        gain_two = jnp.sum(grad_middle * normed_two, axis=0, keepdims=True)
        gain_three = jnp.sum(lifted_grad * normed_three, axis=0, keepdims=True)
        return grad_middle, grad_branch, gain_two, gain_three

    down_part = (down_kept + down_got.astype(f32)).astype(b16)
    grad_w_down = exchange(down_part, "dp")
    gate_got = swapped(gate_sent, "context", 1)
    grad_middle, grad_branch, grad_gain_two, grad_gain_three = fused(
        middle_back, (), own_cotangent, gains, scale_two, normed_two, scale_three, normed_three, *terms
    )
    grad_branch, grad_w_down, gate_got = together(grad_branch, grad_w_down, gate_got)
    gate_part = (gate_kept + gate_got.astype(f32)).astype(b16)


    def row_blocks(left, right):
        return row_grad(left, right).reshape(n, deep, HEAD_SIZE)

    grad_w_gate = exchange(gate_part, "dp")
    up_got = swapped(after(up_sent, gate_got), "context", 1)
    grad_branch = spread_group(grad_branch)
    out_blocks = row_blocks(grad_branch, mixed)
    grad_query_pre, kept, sent = attend_back(
        grad_branch, w_out, keys, values, queries, probs, bent, (cosine_table, sine_table), side
    )
    query_blocks = row_blocks(lifted_one, grad_query_pre)
    up_got, kept = together(up_got, kept)
    up_part = (up_kept + up_got.astype(f32)).astype(b16)
    grad_w_up = exchange(after(up_part, grad_w_gate), "dp")
    out_blocks, query_blocks, output = together(
        after(out_blocks, grad_w_gate), query_blocks, output
    )
    kept = kept.reshape(reach + 1, group, HEAD_SIZE)
    sent = sent.reshape(reach + 1, group, HEAD_SIZE)

    def full(kept, got):
        return kept + got.astype(f32)

    slots = [
        fused(two_sided if slot < reach else full, (), kept[slot], swapped(sent[slot], "context", 1))
        for slot in range(reach + 1)
    ]
    grad_w_out = ring_summed(out_blocks)
    terms = [slots[reach]]
    for steps in range(reach, 0, -1):
        terms.append(shifted(slots[reach - steps], "dp", -steps))
    terms, grad_w_up, grad_w_out = together(terms, grad_w_up, grad_w_out)

    def unturned(is_first, cosine, sine, *terms):
        total = added(terms)
        return jnp.where(is_first, rotate_back(total, cosine, sine), total).astype(b16)

    mine = fused(unturned, (is_first,), cosine_table, sine_table, *terms)
    pair_blocks = row_blocks(lifted_one, mine)

    def first_product(low_core, tokens, query_grad, query_in, pair_grad, pair_in):
        out = dot_nt(query_grad, query_in) + dot_nt(pair_grad, pair_in)
        values = tokens.astype(f32)
        gain = jnp.sum(out * (values * rms_scale(values)), axis=0, keepdims=True)
        return *core_parted(low_core, out, sub), gain

    kept, sent, grad_gain_one = fused(
        first_product,
        (low_core,),
        group_tokens,
        grad_query_pre,
        query_in,
        after(mine, pair_blocks),
        pair_in,
    )
    first_grad = collect_halves(kept, sent)

    def first_back(own_tokens, gains, grad_middle, *halves):
        first_grad = halves_summed(*halves)
        values = own_tokens.astype(f32)
        scale = rms_scale(values)
        return (grad_middle + rms_back(first_grad * gains[:1], values * scale, scale)).astype(b16)

    grad_inputs = fused(first_back, (), own_tokens, gains, grad_middle, *first_grad)
    grad_gains = jnp.concatenate(
        [grad_gain_one, grad_gain_two, grad_gain_three, grad_gain_four], axis=0
    )

    def halves(total):
        kept, sent = picked(is_first, (total[: deep // 2], total[deep // 2 : deep]))
        return kept, swapped(sent.astype(b16), "context", 1).astype(f32)

    grad_gains = after(grad_gains, grad_inputs)
    grad_gains = grad_gains + swapped(grad_gains, "tensor", 2)
    grad_gains = grad_gains + swapped(grad_gains, "tensor", 1)
    grad_w_query = ring_summed(after(query_blocks, *terms), grad_inputs, grad_gains)
    grad_gains = jnp.transpose(grad_gains.reshape(4, n, 2, deep // 2), (2, 1, 0, 3))
    grad_gains, sent = picked(is_first, (grad_gains[0], grad_gains[1]))
    grad_gains = ring_summed(grad_gains + swapped(sent, "context", 1))
    grad_pair = ring_summed(pair_blocks, grad_inputs)
    grad_inputs = spread_lanes(grad_inputs).astype(f32)
    grad_w_out = jnp.concatenate(picked(is_first, halves(grad_w_out)), axis=1).T
    grad_w_query = jnp.concatenate(picked(is_first, halves(grad_w_query)), axis=1)
    grad_w_key, grad_w_value = picked(is_first, halves(grad_pair))
    grad_w_down, grad_w_gate, grad_w_up = after(
        (grad_w_down, grad_w_gate, grad_w_up), mine
    )
    grad_w_down = side_by_side(grad_w_down).T
    grad_w_gate = side_by_side(grad_w_gate)
    grad_w_up = side_by_side(grad_w_up)
    return (
        output,
        grad_inputs,
        grad_w_query,
        grad_w_key,
        grad_w_value,
        grad_w_out,
        grad_w_gate,
        grad_w_up,
        grad_w_down,
        grad_gains[0],
        grad_gains[1],
        grad_gains[2],
        grad_gains[3],
    )


def solution(mesh):
    return jax.shard_map(
        on_device,
        mesh=mesh,
        in_specs=(
            P(("dp", "context"), None),
            P(("dp", "context")),
            P("dp", "tensor"),
            P("dp", "tensor"),
            P("dp", "tensor"),
            P("tensor", "dp"),
            P("dp", "tensor"),
            P("dp", "tensor"),
            P("tensor", "dp"),
            P("dp"),
            P("dp"),
            P("dp"),
            P("dp"),
            P(("dp", "context"), None),
        ),
        out_specs=(
            P(("dp", "context"), None),
            P(("dp", "context"), None),
            P(("dp", "context"), "tensor"),
            P(("dp", "context"), "tensor"),
            P(("dp", "context"), "tensor"),
            P("tensor", ("dp", "context")),
            P(("dp", "context"), "tensor"),
            P(("dp", "context"), "tensor"),
            P("tensor", ("dp", "context")),
            P(("dp", "context")),
            P(("dp", "context")),
            P(("dp", "context")),
            P(("dp", "context")),
        ),
        check_vma=False,
    )
```

```python
import math

import jax
import jax.numpy as jnp
from jax import lax
from jax.experimental import pallas as pl
from jax.experimental.pallas import tpu as pltpu
from jax.sharding import PartitionSpec as P

HEAD_SIZE = 256
SLIDE_WINDOW = 4096


eps = 1e-06
softcap = 50.0
negative = -1e30
f32 = jnp.float32
b16 = jnp.bfloat16


def rms_scale(value_rows):
    return lax.rsqrt(jnp.mean(value_rows * value_rows, axis=-1, keepdims=True) + eps)


def rms_back(grad, normed, scale):
    return scale * (grad - normed * jnp.mean(grad * normed, axis=-1, keepdims=True))


def rotary_tables(positions):
    inverse = 1.0 / 10000.0 ** (jnp.arange(0, HEAD_SIZE, 2, dtype=f32) / HEAD_SIZE)
    angles = positions.astype(f32)[:, None] * inverse[None, :]
    return (jnp.cos(angles), jnp.sin(angles))


def apply_rotary(value_rows, cosine_table, sine_table):
    half = value_rows.shape[-1] // 2
    first, second = value_rows[:, :half], value_rows[:, half:]
    return jnp.concatenate(
        [first * cosine_table - second * sine_table, second * cosine_table + first * sine_table],
        axis=-1,
    )


def rotate_back(grads, cosine_table, sine_table):
    return apply_rotary(grads, cosine_table, -sine_table)


def gated(gate_value, up_value):
    return jax.nn.gelu(gate_value, approximate=True) * up_value


def exchange(blocks, axis):
    return lax.all_to_all(blocks, axis, 0, 0, tiled=True)


def gathered(block, axis):
    count = lax.axis_size(axis)
    return exchange(jnp.broadcast_to(block[None], (count,) + block.shape), axis)


def swapped(value, axis, bit):
    count = lax.axis_size(axis)
    return lax.ppermute(value, axis, [(place, place ^ bit) for place in range(count)])


def passed_on(value, steps, way):
    n = lax.axis_size("dp")
    pairs = [(s, s + 1) for s in range(steps - 1, n - 1)]
    if way < 0:
        pairs = [(n - 1 - s, n - 1 - t) for s, t in pairs]
    return lax.ppermute(value, "dp", pairs)


def shifted(value, axis, steps):
    count = lax.axis_size(axis)
    return lax.ppermute(
        value, axis, [(s, s + steps) for s in range(count) if 0 <= s + steps < count]
    )


def summed(blocks):
    return jnp.sum(blocks.astype(f32), axis=0)


def dot(left, right):
    return jnp.dot(left, right, preferred_element_type=f32)


def dot_nt(left, right):
    return lax.dot_general(left, right, (((1,), (1,)), ((), ())), preferred_element_type=f32)


def dot_tn(left, right):
    return lax.dot_general(left, right, (((0,), (0,)), ((), ())), preferred_element_type=f32)


def rotated(value, steps):
    n = lax.axis_size("dp")
    return lax.ppermute(value, "dp", [(s, (s + steps) % n) for s in range(n)])


def picked(first, pair):
    low, high = pair
    return jnp.where(first, low, high), jnp.where(first, high, low)


def after(value, *earlier):
    return lax.optimization_barrier((value,) + earlier)[0]


def ring_blocks(block):
    n = lax.axis_size("dp")
    return [block] + [rotated(block, steps) for steps in range(1, n)]


def in_order(blocks):
    n = lax.axis_size("dp")
    place = lax.axis_index("dp")
    blocks = [blocks[-j % n] for j in range(n)]
    for bit in range((n - 1).bit_length()):
        shift = 1 << bit
        odd = (place >> bit) % 2 == 1
        blocks = [jnp.where(odd, blocks[(j - shift) % n], blocks[j]) for j in range(n)]
    return jnp.stack(blocks)


def ring_summed(blocks, *earlier):
    n = lax.axis_size("dp")
    place = lax.axis_index("dp")
    total = lax.dynamic_index_in_dim(blocks, place, 0, keepdims=False).astype(f32)
    got = [
        rotated(
            lax.dynamic_index_in_dim(blocks, (place + steps) % n, 0, keepdims=False), steps
        )
        for steps in range(1, n)
    ]
    got = after(got, *earlier)
    for block in got:
        total = total + block.astype(f32)
    return total


def unit_blocks(weights, side, n):
    deep, total = weights[0].shape
    units = total // n
    shape = (n, deep // 2, units)
    if deep % 32:
        halves = [lax.dynamic_slice_in_dim(w, side * (deep // 2), deep // 2) for w in weights]
        return [jnp.swapaxes(w.reshape(deep // 2, n, units), 0, 1) for w in halves]

    def kernel(side_ref, *refs):
        for source, target in zip(refs[: len(weights)], refs[len(weights) :]):
            for j in range(n):
                target[j] = source[:, j * units : (j + 1) * units]

    return pl.pallas_call(
        kernel,
        grid_spec=pltpu.PrefetchScalarGridSpec(
            num_scalar_prefetch=1,
            grid=(1,),
            in_specs=[pl.BlockSpec((deep // 2, total), lambda g, s: (s[0], 0))] * len(weights),
            out_specs=[pl.BlockSpec(shape, lambda g, s: (0, 0, 0))] * len(weights),
        ),
        out_shape=[jax.ShapeDtypeStruct(shape, w.dtype) for w in weights],
        compiler_params=pltpu.CompilerParams(vmem_limit_bytes=48 << 20),
        name="unit_blocks",
    )(side.astype(jnp.int32).reshape(1), *weights)


def side_by_side(blocks):
    n, rows, units = blocks.shape
    if rows % 16:
        return jnp.swapaxes(blocks, 0, 1).reshape(rows, n * units).astype(f32)

    def kernel(source, target):
        for j in range(n):
            target[:, j * units : (j + 1) * units] = source[j].astype(f32)

    return pl.pallas_call(
        kernel,
        out_shape=jax.ShapeDtypeStruct((rows, n * units), f32),
        compiler_params=params(16),
        name="side_by_side",
    )(blocks)


def bits():
    lane = lax.axis_index("tensor")
    return lax.axis_index("context") == 0, lane < 2, lane % 2 == 0


AXES = (("context", 1), ("tensor", 2), ("tensor", 1))


def join(own, step, axis):
    low, high = picked(bits()[step], (own, swapped(own, *AXES[step])))
    return jnp.stack([low, high], axis=axis)


def fold(partial, step, axis):
    low = lax.index_in_dim(partial, 0, axis, keepdims=False)
    high = lax.index_in_dim(partial, 1, axis, keepdims=False)
    kept, sent = picked(bits()[step], (low, high))
    return kept + swapped(sent.astype(b16), *AXES[step]).astype(f32)


def half_sent(partial, step, axis):
    low = lax.index_in_dim(partial, 0, axis, keepdims=False)
    high = lax.index_in_dim(partial, 1, axis, keepdims=False)
    kept, sent = picked(bits()[step], (low, high))
    return kept, swapped(sent.astype(b16), *AXES[step])


def collect_group(partial, sub, *earlier):
    width = partial.shape[-1]
    partial = after(fold(partial.reshape(2, 2, 2, sub, width), 2, 2), *earlier)
    left, right = partial[..., : width // 2], partial[..., width // 2 :]
    left = fold(fold(left, 0, 0), 1, 0)
    right = fold(fold(right, 1, 1), 0, 0)
    return jnp.concatenate([left, right], axis=-1)


SMEM = pltpu.SMEM
VMEM = pltpu.VMEM


def params(megabytes=48):
    return pltpu.CompilerParams(vmem_limit_bytes=megabytes << 20)


def scalar(value):
    return value.astype(jnp.int32).reshape(1)


def whole(shape):
    return pl.BlockSpec(shape, lambda *_: (0,) * len(shape))


def fused(function, flags, *args):
    shapes = jax.eval_shape(function, *flags, *args)
    leaves, tree = jax.tree.flatten(shapes)
    size = sum(math.prod(v.shape) * v.dtype.itemsize for v in (*args, *leaves))
    if size > 32 << 20:
        return function(*flags, *args)
    count = len(flags)

    def kernel(*refs):
        given = [ref[0] == 1 for ref in refs[:count]]
        given += [ref[...] for ref in refs[count : count + len(args)]]
        results = jax.tree.leaves(function(*given))
        for ref, result in zip(refs[count + len(args) :], results):
            ref[...] = result

    out = pl.pallas_call(
        kernel,
        in_specs=[pl.BlockSpec(memory_space=SMEM)] * count
        + [pl.BlockSpec(memory_space=VMEM)] * len(args),
        out_specs=[pl.BlockSpec(memory_space=VMEM)] * len(leaves),
        out_shape=leaves,
        compiler_params=params(8 + (size >> 20)),
        name="fused_" + getattr(function, "__name__", "part").strip("<>_"),
    )(*[scalar(flag) for flag in flags], *args)
    return jax.tree.unflatten(tree, out)


def join_kernel(own, step, axis):
    return put_together(own, swapped(own, *AXES[step]), bits()[step], axis)


def put_together(own, other, first, axis):
    if own.ndim < 2 or own.shape[-2] % 16:
        return jnp.stack(picked(first, (own, other)), axis=axis)
    shape = own.shape[:axis] + (2,) + own.shape[axis:]

    def kernel(place, own_ref, other_ref, out):
        lead = (slice(None),) * axis
        out[(*lead, place[0])] = own_ref[...]
        out[(*lead, 1 - place[0])] = other_ref[...]

    return pl.pallas_call(
        kernel,
        in_specs=[pl.BlockSpec(memory_space=SMEM)] + [pl.BlockSpec(memory_space=VMEM)] * 2,
        out_specs=pl.BlockSpec(memory_space=VMEM),
        out_shape=jax.ShapeDtypeStruct(shape, own.dtype),
        compiler_params=params(8),
        name="join",
    )(1 - scalar(first), own, other)


def parted(first, low, high):
    kept, sent = picked(first, (low, high))
    return kept, sent.astype(b16)


def core_parted(low_core, out, sub):
    parts = [out[k * sub : (k + 1) * sub] for k in range(8)]
    pairs = [parted(low_core, parts[2 * k], parts[2 * k + 1]) for k in range(4)]
    return tuple(
        jnp.concatenate([pair[which] for pair in pairs], axis=0).reshape(2, 2, sub, -1)
        for which in range(2)
    )


def collect_halves(kept, sent, *earlier):
    half = kept.shape[-1] // 2
    context, high, low = bits()

    def halve(context, high, kept, got):
        total = kept + got.astype(f32)
        left, right = total[..., :half], total[..., half:]
        left = parted(context, left[0], left[1])
        right = parted(high, right[:, 0], right[:, 1])
        return *left, *right

    def again(context, high, left, left_got, right, right_got):
        left = left + left_got.astype(f32)
        right = right + right_got.astype(f32)
        return *parted(high, left[0], left[1]), *parted(context, right[0], right[1])

    got = swapped(sent, *AXES[2])
    left, left_sent, right, right_sent = fused(halve, (context, high), kept, got)
    left_sent, right_sent = after((left_sent, right_sent), *earlier)
    left_got, right_got = swapped(left_sent, *AXES[0]), swapped(right_sent, *AXES[1])
    left, left_sent, right, right_sent = fused(
        again, (context, high), left, left_got, right, right_got
    )
    return left, swapped(left_sent, *AXES[1]), right, swapped(right_sent, *AXES[0])


def halves_summed(left, left_got, right, right_got):
    return jnp.concatenate([left + left_got.astype(f32), right + right_got.astype(f32)], axis=-1)


def side_by_side_columns(left, right):
    return jnp.concatenate([left, right], axis=-1)


def spread_group(block):
    width = block.shape[-1]
    left, right = block[:, : width // 2], block[:, width // 2 :]
    left = join_kernel(join_kernel(left, 0, 0), 1, 1)
    right = join_kernel(join_kernel(right, 1, 0), 0, 0)
    return join_kernel(fused(side_by_side_columns, (), left, right), 2, 2).reshape(-1, width)


def spread_lanes(block):
    return join_kernel(join_kernel(block, 1, 0), 2, 1).reshape(-1, block.shape[-1])


def row_grad(left, right):
    width = left.shape[1]
    step = 384

    def kernel(left_ref, right_ref, out):
        for start in range(0, width, step):
            here = slice(start, start + step)
            out[here, :] = dot_tn(left_ref[:, here], right_ref[...]).astype(b16)

    return pl.pallas_call(
        kernel,
        out_shape=jax.ShapeDtypeStruct((width, right.shape[1]), b16),
        compiler_params=params(16),
        name="row_grad",
    )(left, right)


def attend_back(rows, w_out, keys, values, queries, probs, bent, tables, side):
    group, width = rows.shape
    span, size = keys.shape
    block = 128
    steps = group // block

    def kernel(
        side_ref, rows_ref, out_ref, key_ref, value_ref, query_ref, probs_ref, bent_ref, cos_ref, sin_ref,
        query_grad, kept, sent, key_sum, value_sum,
    ):
        step = pl.program_id(0)
        mixed = dot(rows_ref[...], out_ref[...]).astype(b16)
        grads = dot_nt(mixed, value_ref[...])
        probs = probs_ref[...]
        bent = bent_ref[...]
        grads = probs * (grads - jnp.sum(probs * grads, axis=-1, keepdims=True))
        grads = (grads * (1.0 - bent * bent)).astype(b16)
        turned = rotate_back(dot(grads, key_ref[...]), cos_ref[...], sin_ref[...])
        query_grad[...] = (turned * HEAD_SIZE ** (-0.5)).astype(b16)
        key_part = dot_tn(grads, query_ref[...])
        value_part = dot_tn(probs.astype(b16), mixed)

        @pl.when(step == 0)
        def _():
            key_sum[...] = key_part
            value_sum[...] = value_part

        @pl.when(step > 0)
        def _():
            key_sum[...] += key_part
            value_sum[...] += value_part

        @pl.when((step == steps - 1) & (side_ref[0] == 0))
        def _():
            kept[...] = key_sum[...]
            sent[...] = value_sum[...].astype(b16)

        @pl.when((step == steps - 1) & (side_ref[0] == 1))
        def _():
            kept[...] = value_sum[...]
            sent[...] = key_sum[...].astype(b16)

    def by_rows(columns):
        return pl.BlockSpec((block, columns), lambda g: (g, 0))

    return pl.pallas_call(
        kernel,
        grid=(steps,),
        in_specs=[
            pl.BlockSpec(memory_space=SMEM),
            by_rows(width),
            whole((width, size)),
            whole((span, size)),
            whole((span, size)),
            by_rows(size),
            by_rows(span),
            by_rows(span),
            by_rows(size // 2),
            by_rows(size // 2),
        ],
        out_specs=[by_rows(size), whole((span, size)), whole((span, size))],
        out_shape=[
            jax.ShapeDtypeStruct((group, size), b16),
            jax.ShapeDtypeStruct((span, size), f32),
            jax.ShapeDtypeStruct((span, size), b16),
        ],
        scratch_shapes=[pltpu.VMEM((span, size), f32)] * 2,
        compiler_params=params(),
        name="attend_back",
    )(scalar(side), rows, w_out, keys, values, queries, probs, bent, *tables)


def together(*values):
    return lax.optimization_barrier(values)


def added(terms):
    total = terms[0].astype(f32)
    for term in terms[1:]:
        total = total + term.astype(f32)
    return total


def spread_chunk(block, *earlier):
    block = jnp.concatenate([block, swapped(block, "tensor", 2)], axis=0)
    block = after(block, *earlier)
    return jnp.concatenate([block, swapped(block, "tensor", 1)], axis=0)


def folded(partial, bit):
    half = partial.shape[0] // 2
    return partial[:half] + swapped(partial[half:].astype(b16), "tensor", bit).astype(f32)


def pipelined(block, work):
    n = lax.axis_size("dp")
    sub = block.shape[0]
    groups = [[0], [1, n - 1], list(range(2, n - 1))] if n > 3 else [[0], list(range(1, n))]
    rows, partial, rest = [], [], []
    sent = block
    for group in groups:
        got = [rotated(sent, steps) if steps else block for steps in group]
        if group[0]:
            sent = after(block, *got)
        rows.append(got)
    near = rows[1]
    for number, got in enumerate(rows):
        got = jnp.concatenate(got, axis=0) if len(got) > 1 else got[0]
        rows[number] = spread_chunk(got, *partial[:1])
        first, *others = work(number, after(rows[number], *partial[-1:]), *near)
        partial.append(first)
        rest.append(others)

    terms, earlier = [], []
    for number in list(range(1, len(groups))) + [0]:
        back = after(folded(partial[number], 1), *earlier)
        back = folded(back, 2)
        earlier = [back]
        for place, steps in enumerate(groups[number]):
            part = back[place * sub : (place + 1) * sub]
            terms.append(rotated(part.astype(b16), -steps) if steps else part)
    return rows, terms, list(zip(*rest)), partial + earlier


def on_device(
    tokens,
    segments,
    w_query,
    key_weight,
    value_weight,
    w_output,
    w_gate,
    w_up,
    w_down,
    pre_attn_gain,
    post_attn_gain,
    pre_ffw_gain,
    post_ffw_gain,
    cotangent,
):
    n = lax.axis_size("dp")
    place = lax.axis_index("dp")
    side = lax.axis_index("context")
    lane = lax.axis_index("tensor")
    lanes = lax.axis_size("tensor")
    rows, width = tokens.shape
    group = 2 * rows
    sub = rows // lanes
    deep = width // n
    reach = min((SLIDE_WINDOW + group - 2) // group, n - 1)
    is_first = side == 0

    def half_of(value, which, axis):
        size = value.shape[axis] // 2
        low = lax.slice_in_dim(value, 0, size, axis=axis)
        high = lax.slice_in_dim(value, size, 2 * size, axis=axis)
        return jnp.where(which == 0, low, high)

    def with_rider(block, values):
        rider = jnp.zeros((16 * HEAD_SIZE - values.size,), b16)
        rider = jnp.concatenate([values.astype(b16).reshape(-1), rider])
        return jnp.concatenate([block, rider.reshape(16, HEAD_SIZE)], axis=0)

    def split_rider(blocks, count):
        size = blocks.shape[1] - 16
        rider = blocks[:, size:].reshape(blocks.shape[0], -1)[:, :count]
        return blocks[:, :size], rider

    gains = jnp.concatenate([pre_attn_gain, post_attn_gain, pre_ffw_gain, post_ffw_gain])
    pair_got = ring_blocks(jnp.where(is_first, key_weight, value_weight))
    group_tokens = join(tokens, 0, 0).reshape(group, width)
    segment_pair = join(segments[None].astype(b16), 0, 0)
    gains = in_order(ring_blocks(after(gains, segment_pair)))
    pair_in = in_order(pair_got)
    pair_in = pair_in.reshape(width, HEAD_SIZE)
    gains = 1.0 + jnp.swapaxes(gains.reshape(n, 4, deep), 0, 1).reshape(4, width).astype(f32)
    normed_one = group_tokens.astype(f32)
    normed_one = normed_one * rms_scale(normed_one)
    lifted_one = (normed_one * gains[0]).astype(b16)
    positions = place * group + jnp.arange(group, dtype=jnp.int32)
    cosine_table, sine_table = rotary_tables(positions)
    mine = dot(lifted_one, pair_in)
    mine = jnp.where(is_first, apply_rotary(mine, cosine_table, sine_table), mine).astype(b16)
    mine = [mine] + [shifted(mine, "dp", steps) for steps in range(1, reach + 1)]
    query_got = ring_blocks(after(with_rider(half_of(w_query, side, 1), segment_pair), mine[0]))
    query_in, all_segments = split_rider(in_order(query_got), group)
    query_in = query_in.reshape(width, HEAD_SIZE)
    all_segments = all_segments.reshape(-1).astype(jnp.int32)
    out_got = ring_blocks(after(half_of(w_output.T, side, 1), *mine))
    w_out = in_order(out_got).reshape(width, HEAD_SIZE)

    units = w_gate.shape[1] // n
    gate_got, up_got, down_got = unit_blocks([w_gate, w_up, w_down.T], side, n)
    gate_got = exchange(after(gate_got, *mine), "dp")
    up_got = exchange(after(up_got, gate_got), "dp")
    down_got = exchange(after(down_got, up_got), "dp")
    gate_other, up_other, down_other = [
        swapped(got, "context", 1) for got in (gate_got, up_got, down_got)
    ]

    def both_halves(own, other):
        return put_together(own, other, is_first, 1).reshape(width, units)

    theirs = [swapped(block, "context", 1) for block in mine]
    mine = jnp.concatenate(mine[::-1], axis=0)
    theirs = jnp.concatenate(theirs[::-1], axis=0)
    keys = jnp.where(is_first, mine, theirs)
    values = jnp.where(is_first, theirs, mine)
    queries = (
        apply_rotary(dot(lifted_one, query_in), cosine_table, sine_table) * HEAD_SIZE ** (-0.5)
    ).astype(b16)
    span = (reach + 1) * group
    key_positions = (place - reach) * group + jnp.arange(span, dtype=jnp.int32)
    padded = jnp.concatenate([jnp.full((reach * group,), -1, jnp.int32), all_segments])
    key_segments = lax.dynamic_slice_in_dim(padded, place * group, span)
    query_segments = key_segments[reach * group :]
    valid = (key_positions[None, :] <= positions[:, None]) & (
        positions[:, None] - key_positions[None, :] < SLIDE_WINDOW
    )
    valid = valid & (key_positions[None, :] >= 0)
    valid = valid & (key_segments[None, :] == query_segments[:, None])
    bent = jnp.tanh(dot_nt(queries, keys) / softcap)
    masked = jnp.where(valid, softcap * bent, negative)
    weights = jnp.exp(masked - jnp.max(masked, axis=-1, keepdims=True))
    probs = weights / jnp.sum(weights, axis=-1, keepdims=True)
    probs_low = probs.astype(b16)
    mixed = dot(after(probs_low, gate_got, *out_got), values).astype(b16)
    low_core = bits()[2]

    def out_product(low_core, mixed, w_out):
        return core_parted(low_core, dot_nt(mixed, w_out), sub)

    branch = collect_halves(*fused(out_product, (low_core,), mixed, w_out), gate_other)
    branch = after(halves_summed(*branch), up_got, gate_other)

    own_tokens = lax.dynamic_slice_in_dim(tokens, lane * sub, sub)
    own_cotangent = lax.dynamic_slice_in_dim(cotangent, lane * sub, sub)
    grad_out = own_cotangent.astype(f32)
    scale_two = rms_scale(branch)
    normed_two = branch * scale_two
    middle = own_tokens.astype(f32) + normed_two * gains[1]
    scale_three = rms_scale(middle)
    normed_three = middle * scale_three
    lifted_two = after((normed_three * gains[2]).astype(b16), down_got, up_other)
    gate_w = both_halves(gate_got, gate_other)
    up_w = both_halves(up_got, up_other)

    def feed(number, chunk, *arrived):
        down_w = both_halves(down_got, after(down_other, *arrived))
        gate = dot(chunk, gate_w)
        upper = dot(chunk, up_w)
        hidden = gated(gate, upper).astype(b16)
        return dot_nt(hidden, down_w), gate, upper, hidden

    lifted_two, terms, (gate, upper, hidden), unused = pipelined(lifted_two, feed)
    down = added(terms)
    scale_four = rms_scale(down)
    normed_four = down * scale_four
    output = (middle + normed_four * gains[3]).astype(b16)

    grad_gain_four = jnp.sum(grad_out * normed_four, axis=0, keepdims=True)
    def unit_grad(left, right):
        partial = dot_tn(jnp.concatenate(left, axis=0), jnp.concatenate(right, axis=0))
        return partial.reshape(n, 2, deep // 2, units)

    grad_down = rms_back(grad_out * gains[3], normed_four, scale_four).astype(b16)
    down_w = both_halves(down_got, down_other)

    def feed_back(number, chunk, *arrived):
        unused, pull = jax.vjp(gated, gate[number], upper[number])
        grad_gate, grad_upper = [side.astype(b16) for side in pull(dot(chunk, down_w))]
        partial = dot_nt(grad_gate, gate_w) + dot_nt(grad_upper, up_w)
        return partial, grad_gate, grad_upper

    grad_down, terms, (grad_gate, grad_upper), partial = pipelined(grad_down, feed_back)
    output = spread_lanes(after(output, grad_down[0]))
    down_sum = unit_grad(grad_down, after(hidden, partial[-3]))
    down_kept, down_got = half_sent(down_sum, 0, 1)

    def both_parts(total):
        kept, sent = picked(is_first, (total[:, 0], total[:, 1]))
        return kept, sent.astype(b16)

    gate_sum = unit_grad(lifted_two, after(grad_gate, partial[-1]))
    up_sum = unit_grad(lifted_two, after(grad_upper, partial[-1]))
    gate_kept, gate_sent = both_parts(gate_sum)
    up_kept, up_sent = both_parts(up_sum)
    terms, down_got, gate_sent = together(terms, down_got, gate_sent)

    def two_sided(kept, got):
        return (kept + got.astype(f32)).astype(b16)

    def middle_back(cotangent, gains, scale_two, normed_two, scale_three, normed_three, *terms):
        grad_out = cotangent.astype(f32)
        lifted_grad = added(terms)
        grad_middle = grad_out + rms_back(lifted_grad * gains[2:3], normed_three, scale_three)
        grad_branch = rms_back(grad_middle * gains[1:2], normed_two, scale_two).astype(b16)
        gain_two = jnp.sum(grad_middle * normed_two, axis=0, keepdims=True)
        gain_three = jnp.sum(lifted_grad * normed_three, axis=0, keepdims=True)
        return grad_middle, grad_branch, gain_two, gain_three

    down_part = (down_kept + down_got.astype(f32)).astype(b16)
    grad_w_down = exchange(down_part, "dp")
    gate_got = swapped(gate_sent, "context", 1)
    grad_middle, grad_branch, grad_gain_two, grad_gain_three = fused(
        middle_back, (), own_cotangent, gains, scale_two, normed_two, scale_three, normed_three, *terms
    )
    grad_branch, grad_w_down, gate_got = together(grad_branch, grad_w_down, gate_got)
    gate_part = (gate_kept + gate_got.astype(f32)).astype(b16)


    def row_blocks(left, right):
        return row_grad(left, right).reshape(n, deep, HEAD_SIZE)

    grad_w_gate = exchange(gate_part, "dp")
    up_got = swapped(after(up_sent, gate_got), "context", 1)
    grad_branch = spread_group(grad_branch)
    out_blocks = row_blocks(grad_branch, mixed)
    grad_query_pre, kept, sent = attend_back(
        grad_branch, w_out, keys, values, queries, probs, bent, (cosine_table, sine_table), side
    )
    query_blocks = row_blocks(lifted_one, grad_query_pre)
    up_got, kept = together(up_got, kept)
    up_part = (up_kept + up_got.astype(f32)).astype(b16)
    grad_w_up = exchange(after(up_part, grad_w_gate), "dp")
    out_blocks, query_blocks, output = together(
        after(out_blocks, grad_w_gate), query_blocks, output
    )
    kept = kept.reshape(reach + 1, group, HEAD_SIZE)
    sent = sent.reshape(reach + 1, group, HEAD_SIZE)

    def full(kept, got):
        return kept + got.astype(f32)

    slots = [
        fused(two_sided if slot < reach else full, (), kept[slot], swapped(sent[slot], "context", 1))
        for slot in range(reach + 1)
    ]
    grad_w_out = ring_summed(out_blocks)
    terms = [slots[reach]]
    for steps in range(reach, 0, -1):
        terms.append(shifted(slots[reach - steps], "dp", -steps))
    terms, grad_w_up, grad_w_out = together(terms, grad_w_up, grad_w_out)

    def unturned(is_first, cosine, sine, *terms):
        total = added(terms)
        return jnp.where(is_first, rotate_back(total, cosine, sine), total).astype(b16)

    mine = fused(unturned, (is_first,), cosine_table, sine_table, *terms)
    pair_blocks = row_blocks(lifted_one, mine)

    def first_product(low_core, tokens, query_grad, query_in, pair_grad, pair_in):
        out = dot_nt(query_grad, query_in) + dot_nt(pair_grad, pair_in)
        values = tokens.astype(f32)
        gain = jnp.sum(out * (values * rms_scale(values)), axis=0, keepdims=True)
        return *core_parted(low_core, out, sub), gain

    kept, sent, grad_gain_one = fused(
        first_product,
        (low_core,),
        group_tokens,
        grad_query_pre,
        query_in,
        after(mine, pair_blocks),
        pair_in,
    )
    first_grad = collect_halves(kept, sent)

    def first_back(own_tokens, gains, grad_middle, *halves):
        first_grad = halves_summed(*halves)
        values = own_tokens.astype(f32)
        scale = rms_scale(values)
        return (grad_middle + rms_back(first_grad * gains[:1], values * scale, scale)).astype(b16)

    grad_inputs = fused(first_back, (), own_tokens, gains, grad_middle, *first_grad)
    grad_gains = jnp.concatenate(
        [grad_gain_one, grad_gain_two, grad_gain_three, grad_gain_four], axis=0
    )

    def halves(total):
        kept, sent = picked(is_first, (total[: deep // 2], total[deep // 2 : deep]))
        return kept, swapped(sent.astype(b16), "context", 1).astype(f32)

    grad_gains = after(grad_gains, grad_inputs)
    grad_gains = grad_gains + swapped(grad_gains, "tensor", 2)
    grad_gains = grad_gains + swapped(grad_gains, "tensor", 1)
    grad_w_query = ring_summed(after(query_blocks, *terms), grad_inputs, grad_gains)
    grad_gains = jnp.transpose(grad_gains.reshape(4, n, 2, deep // 2), (2, 1, 0, 3))
    grad_gains, sent = picked(is_first, (grad_gains[0], grad_gains[1]))
    grad_gains = ring_summed(grad_gains + swapped(sent, "context", 1))
    grad_pair = ring_summed(pair_blocks, grad_inputs)
    grad_inputs = spread_lanes(grad_inputs).astype(f32)
    grad_w_out = jnp.concatenate(picked(is_first, halves(grad_w_out)), axis=1).T
    grad_w_query = jnp.concatenate(picked(is_first, halves(grad_w_query)), axis=1)
    grad_w_key, grad_w_value = picked(is_first, halves(grad_pair))
    grad_w_down, grad_w_gate, grad_w_up = after(
        (grad_w_down, grad_w_gate, grad_w_up), mine
    )
    grad_w_down = side_by_side(grad_w_down).T
    grad_w_gate = side_by_side(grad_w_gate)
    grad_w_up = side_by_side(grad_w_up)
    return (
        output,
        grad_inputs,
        grad_w_query,
        grad_w_key,
        grad_w_value,
        grad_w_out,
        grad_w_gate,
        grad_w_up,
        grad_w_down,
        grad_gains[0],
        grad_gains[1],
        grad_gains[2],
        grad_gains[3],
    )


def solution(mesh):
    return jax.shard_map(
        on_device,
        mesh=mesh,
        in_specs=(
            P(("dp", "context"), None),
            P(("dp", "context")),
            P("dp", "tensor"),
            P("dp", "tensor"),
            P("dp", "tensor"),
            P("tensor", "dp"),
            P("dp", "tensor"),
            P("dp", "tensor"),
            P("tensor", "dp"),
            P("dp"),
            P("dp"),
            P("dp"),
            P("dp"),
            P(("dp", "context"), None),
        ),
        out_specs=(
            P(("dp", "context"), None),
            P(("dp", "context"), None),
            P(("dp", "context"), "tensor"),
            P(("dp", "context"), "tensor"),
            P(("dp", "context"), "tensor"),
            P("tensor", ("dp", "context")),
            P(("dp", "context"), "tensor"),
            P(("dp", "context"), "tensor"),
            P("tensor", ("dp", "context")),
            P(("dp", "context")),
            P(("dp", "context")),
            P(("dp", "context")),
            P(("dp", "context")),
        ),
        check_vma=False,
    )
```
